512 devices in a mesh: row: 32 (over y, z_lo), col: 16 (over z_hi, x, core).
Axes of the slice: x: 4, y: 4, z: 16 (z_hi: 2, z_lo: 8; z = z_hi * 8 + z_lo), core: 2. Of those that a mesh axis runs over, the one named last changes fastest.
Arguments:
- amplitudes: float32 [32, 32, 384, 384], P('row', 'col'), may hold values from -6 to 6
- exchange_ints: float32 [32, 32, 384, 384], P('row', 'col'), may hold values from -6 to 6
- virt_fock: float32 [384, 384], replicated, as said below
- intersection: float32 [384, 384], replicated, as said below
- occ_fock: float32 [32, 32], replicated, may hold values from -1.5 to 0.3, as said below
- virt_energy: float32 [384], replicated, may hold values from 1 to 3
- fock_tiles: int32 [3, 3], replicated, may hold values from 0 to 1, as said below
- intersection_tiles: int32 [3, 3], replicated, may hold values from 0 to 1, as said below
- occ_pattern: int32 [32, 32], replicated, may hold values from 0 to 1, as said below
- pair_domain: int32 [32, 32, 3], P('row', 'col'), may hold values 0 or 1
Outputs:
- new_amplitudes: float32 [32, 32, 384, 384], P('row', 'col')
The draws below stay inside these ranges and needn't reach their ends.
Inputs may be any that keep to these rules, and one draw needn't show every extreme that they name: `virt_fock`: symmetric. `intersection`: symmetric. `occ_fock`: diagonal entries between -1.5 and -0.3, the others between -0.3 and 0.3. `fock_tiles`: symmetric, every diagonal tile 1, some off-diagonal tile 0. `intersection_tiles`: symmetric, every diagonal tile 1, some off-diagonal tile 0. `occ_pattern`: 1 on the diagonal, 0 where the two orbitals lie more than 1 apart in index.
All inputs are finite; a program needn't handle non-finite values. No bound on the sum of `pair_domain` on one device may be relied on, other than what follows from the above.
Results may differ from the reference program's by a relative error of at most 0.0001.
Values sent between devices are 32-bit elements; how exact they have to be, the bound alone decides.
A program may use at most 64 MiB of HBM per device.

```python
import math
import jax
import jax.numpy as jnp
from jax import lax

NV = 384
TILE = 128
BAND = 1
ITERS = 2
NO = 32
NT = 3


def symmetric_part(key, spread):
    random_mat = jax.random.normal(key, (NV, NV), jnp.float32)
    return (random_mat + random_mat.T) * (spread / math.sqrt(2.0 * NV))


def draw_virt_fock(key, part):
    key_off, key_diag = jax.random.split(jax.random.fold_in(key, 11))
    off_part = symmetric_part(key_off, 0.5)
    diagonal = jax.random.uniform(key_diag, (NV,), jnp.float32, 1.0, 3.0)
    return off_part + jnp.diag(diagonal)


def draw_intersection(key, part):
    key_off = jax.random.fold_in(key, 23)
    off_part = symmetric_part(key_off, 0.3)
    return off_part + jnp.eye(NV, dtype=jnp.float32)


def draw_occ_fock(key, part):
    key_off, key_diag = jax.random.split(jax.random.fold_in(key, 37))
    off_part = jax.random.uniform(key_off, (NO, NO), jnp.float32, -0.3, 0.3)
    diagonal = jax.random.uniform(key_diag, (NO,), jnp.float32, -1.5, -0.3)
    return jnp.where(jnp.eye(NO, dtype=bool), jnp.diag(diagonal), off_part)


def symmetric_tiles(key):
    key_bits, key_first, key_step = jax.random.split(key, 3)
    random_bits = jax.random.randint(key_bits, (NT, NT), 0, 2)
    positions = jnp.arange(NT)
    upper = positions[:, None] < positions[None, :]
    joined = jnp.where(upper, random_bits, random_bits.T)
    first_tile = jax.random.randint(key_first, (), 0, NT)
    other_tile = (first_tile + jax.random.randint(key_step, (), 1, NT)) % NT
    cleared = (positions[:, None] == first_tile) & (positions[None, :] == other_tile) | (positions[:, None] == other_tile) & (positions[None, :] == first_tile)
    joined = jnp.where(cleared, 0, joined)
    return jnp.where(jnp.eye(NT, dtype=bool), 1, joined).astype(jnp.int32)


def draw_fock_tiles(key, part):
    return symmetric_tiles(jax.random.fold_in(key, 41))


def draw_intersection_tiles(key, part):
    return symmetric_tiles(jax.random.fold_in(key, 43))


def draw_occ_pattern(key, part):
    random_bits = jax.random.randint(jax.random.fold_in(key, 47), (NO, NO), 0, 2)
    positions = jnp.arange(NO)
    distance = jnp.abs(positions[:, None] - positions[None, :])
    return jnp.where(distance == 0, 1, jnp.where(distance <= BAND, random_bits, 0)).astype(jnp.int32)


def plant(entries, key, least, high):
    spot = [jax.random.randint(jax.random.fold_in(key, axis), (), 0, length) for axis, length in enumerate(entries.shape)]
    widest = entries.shape.index(max(entries.shape))
    neighbour = spot[:widest] + [(spot[widest] + 1) % entries.shape[widest]] + spot[widest + 1:]
    return entries.at[tuple(spot)].set(least).at[tuple(neighbour)].set(high)


def block_scale(key, extent, cuts, least, largest):
    level, own = 1.0, jax.random.fold_in(key, 6)
    for dim, shards_of in cuts:
        draws = jnp.exp(jax.random.uniform(jax.random.fold_in(own, dim), (shards_of,), jnp.float32, least / len(cuts), largest / len(cuts)))
        level = level * jnp.repeat(draws, extent[dim] // shards_of).reshape([-1 if axis == dim else 1 for axis in range(len(extent))])
    return level


def normal_values(key, extent, deviation, limit, shards=(), kind=jnp.bfloat16):
    entries = jax.random.normal(key, extent, jnp.float32) * deviation
    if len(shards) > 0:
        entries = block_scale(key, extent, shards, -0.22, 0.18) * entries
    return jnp.clip(entries, min=-limit, max=limit).astype(kind)


def setup_inputs(seed: int = 0) -> dict:
    seeds = jax.random.split(jax.random.key(seed), 11)
    amplitudes = normal_values(seeds[0], (NO, NO, NV, NV), 1.0, 6.0, ((0, 32), (1, 16)), jnp.float32)
    exchange_ints = normal_values(seeds[1], (NO, NO, NV, NV), 1.0, 6.0, ((0, 32), (1, 16)), jnp.float32)
    virt_fock = draw_virt_fock(jax.random.fold_in(seeds[10], 71), 0)
    intersection = draw_intersection(jax.random.fold_in(seeds[10], 71), 0)
    occ_fock = draw_occ_fock(jax.random.fold_in(seeds[10], 71), 0)
    virt_energy = jnp.clip(jax.random.uniform(seeds[5], (NV,), jnp.float32, 1.0, 3.0), 1.0, 3.0)
    fock_tiles = draw_fock_tiles(jax.random.fold_in(seeds[10], 71), 0)
    intersection_tiles = draw_intersection_tiles(jax.random.fold_in(seeds[10], 71), 0)
    occ_pattern = draw_occ_pattern(jax.random.fold_in(seeds[10], 71), 0)
    pair_domain = plant((jax.random.randint(seeds[9], (NO, NO, NT), 0, 4) < 3).astype(jnp.int32), jax.random.fold_in(seeds[9], 1), 0, 1)
    return {"amplitudes": amplitudes, "exchange_ints": exchange_ints, "virt_fock": virt_fock, "intersection": intersection, "occ_fock": occ_fock, "virt_energy": virt_energy, "fock_tiles": fock_tiles, "intersection_tiles": intersection_tiles, "occ_pattern": occ_pattern, "pair_domain": pair_domain}


HIGHEST = lax.Precision.HIGHEST


def expand_tiles(tiles):
    return jnp.repeat(jnp.repeat(tiles.astype(jnp.float32), TILE, axis=0), TILE, axis=1)


def sandwich(left_mat, blocks, right_mat):
    partial_value = jnp.einsum('jab,bc->jac', blocks, right_mat, precision=HIGHEST)
    return jnp.einsum('ac,jcb->jab', left_mat, partial_value, precision=HIGHEST)


def reference(amplitudes, exchange_ints, virt_fock, intersection, occ_fock, virt_energy, fock_tiles, intersection_tiles, occ_pattern, pair_domain):
    fock_eff = virt_fock * expand_tiles(fock_tiles)
    over_eff = intersection * expand_tiles(intersection_tiles)
    coupling = occ_fock * occ_pattern.astype(jnp.float32)
    occ_diag = jnp.diagonal(occ_fock)
    domain = jnp.repeat(pair_domain.astype(jnp.float32), TILE, axis=2)
    current = amplitudes
    for iteration in range(ITERS):
        def row_half(pieces):
            blocks, couple_row = pieces
            coupled = jnp.einsum('k,kjab->jab', couple_row, current, precision=HIGHEST)
            return sandwich(fock_eff, blocks, over_eff) - sandwich(over_eff, coupled, over_eff)

        half_resid = lax.map(row_half, (current, coupling))
        mirrored = jnp.transpose(half_resid, (1, 0, 3, 2))
        residual = exchange_ints + half_resid + mirrored

        def row_update(pieces):
            blocks, resid_row, domain_row, occ_value = pieces
            denominator = virt_energy[None, :, None] + virt_energy[None, None, :] - occ_value - occ_diag[:, None, None]
            step_scale = domain_row[:, :, None] * domain_row[:, None, :] / denominator
            return blocks - step_scale * resid_row

        current = lax.map(row_update, (current, residual, domain, occ_diag))
    return current
```

```python
import functools

import jax
import jax.numpy as jnp
from jax import lax
from jax.experimental import pallas as pl
from jax.experimental.pallas import tpu as pltpu
from jax.sharding import PartitionSpec as P

TILE = 128
NT = 3
NV = 384
NCH = 3
CH = NV // NCH
ITERS = 2
MESH = pl.DeviceIdType.MESH
HIGHEST = lax.Precision.HIGHEST


def bit(value, place):
    return (value // (1 << place)) % 2


def xor(*bits):
    total = bits[0]
    for one in bits[1:]:
        total = total + one
    return total % 2


def dot_nt(left, right):
    return lax.dot_general(left, right, (((1,), (1,)), ((), ())), precision=HIGHEST, preferred_element_type=jnp.float32)


def dot_nn(left, right):
    return lax.dot_general(left, right, (((1,), (0,)), ((), ())), precision=HIGHEST, preferred_element_type=jnp.float32)


def kernel(
    x_ref, k_ref, fock_ref, over_ref, occ_ref, ener_ref, ftile_ref, otile_ref, opat_ref, dom_ref,
    out_ref,
    fe, se, mm, x1, hbuf, rbuf, mbuf, gt, dd, gg, scale, ener, vtw,
    hs, hr, l1s, l1r, l2s, l2r,
):
    row = lax.axis_index("row")
    col = lax.axis_index("col")
    y1, y0, a2, a1, a0 = (bit(row, n) for n in (4, 3, 2, 1, 0))
    zh, x1b, x0, core = (bit(col, n) for n in (3, 2, 1, 0))

    def at(y1_, y0_, a2_, a1_, a0_, zh_, x1_, x0_, core_):
        return y1_ * 16 + y0_ * 8 + a2_ * 4 + a1_ * 2 + a0_, zh_ * 8 + x1_ * 4 + x0_ * 2 + core_

    def other(device):
        return jnp.logical_or(device[0] != row, device[1] != col)

    def relay_of(s):
        return at(xor(core, a1), y0, a2, a1, a0, zh, x1b, xor(s, a0, x0, a2), y1)

    def relay_source(t):
        return at(core, y0, a2, a1, a0, zh, x1b, t, xor(y1, a1))

    def final_of(t):
        return at(zh, x1b, t, xor(y1, a1), xor(x0, a0, t, a2), core, y0, a2, a1)

    def final_source(s):
        return at(xor(a1, core), x1b, x0, core, s, y1, y0, xor(a0, s, a2, x0), zh)

    def block_of(ph):
        return xor(a0, ph)

    def slot_of(ph):
        return xor(x0, a2, ph)

    has_below = row > 0
    has_above = row < 31
    below = (jnp.maximum(row - 1, 0), col)
    above = (jnp.minimum(row + 1, 31), col)

    barrier = pltpu.get_barrier_semaphore()

    def greet(device, on):
        @pl.when(on)
        def _():
            pl.semaphore_signal(barrier, inc=1, device_id=device, device_id_type=MESH)

    greet(below, has_below)
    greet(above, has_above)
    count = has_below.astype(jnp.int32) + has_above.astype(jnp.int32)
    for s in range(2):
        for device in (relay_source(s), final_source(s)):
            greet(device, other(device))
        for device in (relay_of(s), final_of(s)):
            count = count + other(device).astype(jnp.int32)

    for ta in range(NT):
        for tb in range(NT):
            rows, cols = pl.ds(ta * TILE, TILE), pl.ds(tb * TILE, TILE)
            fe[rows, cols] = fock_ref[rows, cols] * ftile_ref[ta, tb].astype(jnp.float32)
            se[rows, cols] = over_ref[rows, cols] * otile_ref[ta, tb].astype(jnp.float32)

    pl.semaphore_wait(barrier, count)

    def rows_of(c):
        return pl.ds(c * CH, CH)

    def halo_copies(it, s, c):
        source = x_ref.at[0, s, rows_of(c)] if it == 0 else x1.at[s, rows_of(c)]
        copies = []
        for way, device in ((0, above), (1, below)):
            n = ((it * 2 + way) * 2 + s) * NCH + c
            copies.append(pltpu.make_async_remote_copy(
                src_ref=source, dst_ref=hbuf.at[it, way, s, rows_of(c)], send_sem=hs.at[n], recv_sem=hr.at[n],
                device_id=device, device_id_type=MESH))
        return copies

    def halo_start(it, s, c):
        up, down = halo_copies(it, s, c)

        @pl.when(has_above)
        def _():
            up.start()

        @pl.when(has_below)
        def _():
            down.start()

    def halo_wait_send(it, s, c):
        up, down = halo_copies(it, s, c)

        @pl.when(has_above)
        def _():
            up.wait_send()

        @pl.when(has_below)
        def _():
            down.wait_send()

    def halo_wait_recv(it, s, c):
        up, down = halo_copies(it, s, c)

        @pl.when(has_below)
        def _():
            up.wait_recv()

        @pl.when(has_above)
        def _():
            down.wait_recv()

    def leg(source, target, send, recv, device):
        def remote():
            return pltpu.make_async_remote_copy(
                src_ref=source, dst_ref=target, send_sem=send, recv_sem=recv, device_id=device, device_id_type=MESH)

        def local():
            return pltpu.make_async_copy(source, target, recv)

        return remote, local

    def leg1(it, s, c):
        device = relay_of(s)
        return leg(
            gt.at[it, s, rows_of(c)], rbuf.at[it, x0, rows_of(c)],
            l1s.at[(it * 2 + s) * NCH + c], l1r.at[(it * 2 + x0) * NCH + c], device), other(device)

    def leg2(it, t, c):
        device = final_of(t)
        return leg(
            rbuf.at[it, t, rows_of(c)], mbuf.at[it, a0, rows_of(c)],
            l2s.at[(it * 2 + t) * NCH + c], l2r.at[(it * 2 + a0) * NCH + c], device), other(device)

    def leg_start(pair):
        (remote, local), on = pair

        @pl.when(on)
        def _():
            remote().start()

        @pl.when(jnp.logical_not(on))
        def _():
            local().start()

    def leg_wait_send(pair):
        (remote, _), on = pair

        @pl.when(on)
        def _():
            remote().wait_send()

    def landed(buffer, semaphore):
        pltpu.make_async_copy(buffer, buffer, semaphore).wait()

    for s in range(2):
        for it in range(ITERS):
            @pl.when(jnp.logical_not(has_below))
            def _():
                hbuf[it, 0, s] = jnp.zeros((NV, NV), jnp.float32)

            @pl.when(jnp.logical_not(has_above))
            def _():
                hbuf[it, 1, s] = jnp.zeros((NV, NV), jnp.float32)

    b0, b1 = block_of(0), block_of(1)
    for c in range(NCH):
        halo_start(0, b1, c)
    for c in range(NCH):
        halo_start(0, b0, c)

    prev, succ = jnp.maximum(row - 1, 0), jnp.minimum(row + 1, 31)
    c_own = occ_ref[row, row] * opat_ref[row, row].astype(jnp.float32)
    c_below = occ_ref[row, prev] * opat_ref[row, prev].astype(jnp.float32) * has_below.astype(jnp.float32)
    c_above = occ_ref[row, succ] * opat_ref[row, succ].astype(jnp.float32) * has_above.astype(jnp.float32)
    mm[...] = fe[...] - c_own * se[...]

    def own_part(it, s):
        current = x_ref[0, s] if it == 0 else x1[s]
        dd[s] = dot_nn(dot_nt(se[...], current), mm[...])

    def half_residual(it, s):
        for c in range(NCH):
            halo_wait_recv(it, s, c)
            near = c_below * hbuf[it, 0, s, rows_of(c)] + c_above * hbuf[it, 1, s, rows_of(c)]
            vtw[:, rows_of(c)] = dot_nt(se[...], near)
        for c in range(NCH):
            gt[it, s, rows_of(c)] = dd[s, rows_of(c)] - dot_nn(vtw[rows_of(c)], se[...])
            leg_start(leg1(it, s, c))
        gg[s] = jnp.transpose(gt[it, s])

    def forward(it, t):
        for c in range(NCH):
            landed(rbuf.at[it, t, rows_of(c)], l1r.at[(it * 2 + t) * NCH + c])
            leg_start(leg2(it, t, c))

    def make_scale(s):
        pair = 2 * col + s
        shift = occ_ref[row, row] + occ_ref[pair, pair]
        for ta in range(NT):
            for tb in range(NT):
                rows, cols = pl.ds(ta * TILE, TILE), pl.ds(tb * TILE, TILE)
                both = (dom_ref[0, s, ta] * dom_ref[0, s, tb]).astype(jnp.float32)
                scale[s, rows, cols] = both / (ener[rows, cols] - shift)

    def update(it, s):
        for c in range(NCH):
            rows = rows_of(c)
            landed(mbuf.at[it, s, rows], l2r.at[(it * 2 + s) * NCH + c])
            residual = k_ref[0, s, rows] + gg[s, rows] + mbuf[it, s, rows]
            if it == 0:
                x1[s, rows] = x_ref[0, s, rows] - scale[s, rows] * residual
                halo_start(1, s, c)
            else:
                out_ref[0, s, rows] = x1[s, rows] - scale[s, rows] * residual

    across = jnp.broadcast_to(ener_ref[...], (NV, NV))
    own_part(0, b0)
    ener[...] = across + jnp.transpose(across)
    make_scale(b0)
    make_scale(b1)
    half_residual(0, b0)
    own_part(0, b1)
    forward(0, slot_of(0))
    half_residual(0, b1)
    forward(0, slot_of(1))
    update(0, b0)
    own_part(1, b0)
    update(0, b1)
    own_part(1, b1)
    half_residual(1, b1)
    forward(1, slot_of(1))
    half_residual(1, b0)
    forward(1, slot_of(0))
    update(1, b1)
    update(1, b0)
    for it in range(ITERS):
        for s in range(2):
            for c in range(NCH):
                halo_wait_send(it, s, c)
                leg_wait_send(leg1(it, s, c))
                leg_wait_send(leg2(it, s, c))


def shards(
    amplitudes, exchange_ints, virt_fock, intersection, occ_fock, virt_energy, fock_tiles, intersection_tiles,
    occ_pattern, pair_domain,
):
    vmem, smem = pl.BlockSpec(memory_space=pltpu.VMEM), pl.BlockSpec(memory_space=pltpu.SMEM)
    block = (NV, NV)
    return pl.pallas_call(
        kernel,
        out_shape=jax.ShapeDtypeStruct(amplitudes.shape, jnp.float32),
        in_specs=[vmem, vmem, vmem, vmem, smem, vmem, smem, smem, smem, smem],
        out_specs=vmem,
        scratch_shapes=[
            pltpu.VMEM(block, jnp.float32),
            pltpu.VMEM(block, jnp.float32),
            pltpu.VMEM(block, jnp.float32),
            pltpu.VMEM((2,) + block, jnp.float32),
            pltpu.VMEM((ITERS, 2, 2) + block, jnp.float32),
            pltpu.VMEM((ITERS, 2) + block, jnp.float32),
            pltpu.VMEM((ITERS, 2) + block, jnp.float32),
            pltpu.VMEM((ITERS, 2) + block, jnp.float32),
            pltpu.VMEM((2,) + block, jnp.float32),
            pltpu.VMEM((2,) + block, jnp.float32),
            pltpu.VMEM((2,) + block, jnp.float32),
            pltpu.VMEM(block, jnp.float32),
            pltpu.VMEM(block, jnp.float32),
            pltpu.SemaphoreType.DMA((ITERS * 2 * 2 * NCH,)),
            pltpu.SemaphoreType.DMA((ITERS * 2 * 2 * NCH,)),
            pltpu.SemaphoreType.DMA((ITERS * 2 * NCH,)),
            pltpu.SemaphoreType.DMA((ITERS * 2 * NCH,)),
            pltpu.SemaphoreType.DMA((ITERS * 2 * NCH,)),
            pltpu.SemaphoreType.DMA((ITERS * 2 * NCH,)),
        ],
        compiler_params=pltpu.CompilerParams(collective_id=0, has_side_effects=True, vmem_limit_bytes=48 * 1024 * 1024),
        cost_estimate=pl.CostEstimate(flops=32 * NV * NV * NV, bytes_accessed=24 * NV * NV, transcendentals=0),
    )(
        amplitudes, exchange_ints, virt_fock, intersection, occ_fock, virt_energy.reshape(1, NV), fock_tiles,
        intersection_tiles, occ_pattern, pair_domain,
    )


def solution(mesh):
    in_specs = (
        P("row", "col", None, None),
        P("row", "col", None, None),
        P(),
        P(),
        P(),
        P(),
        P(),
        P(),
        P(),
        P("row", "col", None),
    )
    out_specs = P("row", "col", None, None)
    return jax.shard_map(shards, mesh=mesh, in_specs=in_specs, out_specs=out_specs, check_vma=False)
```

```python
import jax
import jax.numpy as jnp
from jax import lax
from jax.experimental import pallas as pl
from jax.experimental.pallas import tpu as pltpu
from jax.sharding import PartitionSpec as P

TILE = 128
NT = 3
NV = 384
NCH = 3
CH = NV // NCH
ITERS = 2
HEAD = 8
MESH = pl.DeviceIdType.MESH
HIGHEST = lax.Precision.HIGHEST


def bit(value, place):
    return (value // (1 << place)) % 2


def xor(left, right):
    return (left + right) % 2


def xor3(left, right):
    return sum(xor(bit(left, n), bit(right, n)) * (1 << n) for n in range(3))


def less(left, right):
    return (right - left + 7) // 8


def pick(flag, yes, no):
    return flag * yes + (1 - flag) * no


def parts(index):
    return index // 16, bit(index, 3), index % 8


def is_first(i, j):
    p, u, a = parts(i)
    q, v, b = parts(j)
    near = xor(less(b, a), 1 - u)
    return pick(xor(u, v), u, pick(xor(p, q), xor(p, u), near))


def spot(i, j, zh, zl):
    p, u, a = parts(i)
    q, v, b = parts(j)
    m = xor3(a, b)
    return (2 * xor(u, v) + m // 4) * 8 + zl, zh * 8 + (m % 4) * 2 + xor(p, q)


def manager(i, j):
    first = is_first(i, j)
    zh = pick(first, j // 16, i // 16)
    zl = pick(first, i % 8, j % 8)
    return spot(i, j, zh, zl), 1 - first


def in_plane(i, j):
    return spot(i, j, j // 16, i % 8), 1 - is_first(i, j)


def held(row, col):
    y, a, q = row // 8, row % 8, col // 8
    c, d = y // 2, col % 2
    m = 4 * (y % 2) + (col // 2) % 4
    b = xor3(a, m)
    p = xor(q, d)
    diag = (1 - c) * (1 - d) * ((7 - m) // 7)
    same = pick(d, q, less(b, a))
    u = pick(c, 1, same)
    v = (1 - c) * (same + diag)
    one, two = 16 * p + 8 * u + a, 16 * q + 8 * v + b
    partner = y * 8 + b, p * 8 + col % 8
    return (one, pick(diag, one, two)), (two, pick(diag, two, one)), diag, partner


def home(i, j):
    return i, j // 2


def dot_nt(left, right):
    return lax.dot_general(left, right, (((1,), (1,)), ((), ())), precision=HIGHEST, preferred_element_type=jnp.float32)


def dot_nn(left, right):
    return lax.dot_general(left, right, (((1,), (0,)), ((), ())), precision=HIGHEST, preferred_element_type=jnp.float32)


def rows_of(c):
    return pl.ds(c * CH, CH)


def e_rows_of(c):
    return pl.ds(0, CH + HEAD) if c == 0 else pl.ds(HEAD + c * CH, CH)


def tile_of(t):
    return pl.ds(t * TILE, TILE)


def kernel(
    x_ref, k_ref, fock_ref, over_ref, occ_ref, ener_ref, ftile_ref, otile_ref, opat_ref, dom_ref,
    out_ref,
    fe, se, mm, ener, xin, ein, e0, scale, rden, x1, hbuf, gt, dd, vtw, hsum, hout, hin,
    xs, xr, es, er, xs2, xr2, es2, er2, hs, hr, os, orc,
):
    row = lax.axis_index("row")
    col = lax.axis_index("col")

    def other(device):
        return jnp.logical_or(device[0] != row, device[1] != col)

    own = [(row, 2 * col + s) for s in range(2)]
    first_hop = [in_plane(*pair) for pair in own]
    managed_at = [manager(*pair) for pair in own]
    one, two, diag, partner = held(row, col)
    blocks = (one, two)
    relayed = held(*partner)[1]
    targets = []
    for k, l in blocks:
        ways = []
        for step in (1, -1):
            there = jnp.logical_and(k + step >= 0, k + step <= 31)
            device, w = manager(jnp.clip(k + step, 0, 31), l)
            ways.append((device, w, there))
        targets.append(ways)

    barrier = pltpu.get_barrier_semaphore()

    def greet(device, on):
        @pl.when(on)
        def _():
            pl.semaphore_signal(barrier, inc=1, device_id=device, device_id_type=MESH)

    count = jnp.int32(0)
    for device in (home(*one), home(*relayed), partner, managed_at[0][0], managed_at[1][0]):
        greet(device, other(device))
    for device in (first_hop[0][0], first_hop[1][0], partner, home(*one), home(*two)):
        count = count + other(device).astype(jnp.int32)
    for ways in targets:
        for device, _, there in ways:
            greet(device, there)
            count = count + there.astype(jnp.int32)

    for w in range(2):
        for way in range(2):
            @pl.when(jnp.logical_not(targets[w][1 - way][2]))
            def _():
                for it in range(ITERS):
                    hbuf[it, way, w] = jnp.zeros((NV, NV), jnp.float32)

    pl.semaphore_wait(barrier, count)

    def remote(source, target, send, recv, device):
        return pltpu.make_async_remote_copy(
            src_ref=source, dst_ref=target, send_sem=send, recv_sem=recv, device_id=device, device_id_type=MESH)

    def start(args, device):
        @pl.when(other(device))
        def _():
            remote(*args, device).start()

        @pl.when(jnp.logical_not(other(device)))
        def _():
            pltpu.make_async_copy(args[0], args[1], args[3]).start()

    def wait_send(args, device):
        @pl.when(other(device))
        def _():
            remote(*args, device).wait_send()

    def landed(buffer, semaphore):
        pltpu.make_async_copy(buffer, buffer, semaphore).wait()

    def x_hop(s, c):
        device, w = first_hop[s]
        return (x_ref.at[0, s, rows_of(c)], xin.at[2 * w, rows_of(c)], xs.at[s * NCH + c], xr.at[w * NCH + c]), device

    def e_hop(s, c):
        device, w = first_hop[s]
        return (e0.at[s, e_rows_of(c)], ein.at[2 * w, e_rows_of(c)], es.at[s * NCH + c], er.at[w * NCH + c]), device

    def x_relay(c):
        return (xin.at[2, rows_of(c)], xin.at[1, rows_of(c)], xs2.at[c], xr2.at[c]), partner

    def e_relay(c):
        return (ein.at[2, e_rows_of(c)], ein.at[1, e_rows_of(c)], es2.at[c], er2.at[c]), partner

    def x_landed(w, c):
        landed(xin.at[w, rows_of(c)], xr2.at[c] if w else xr.at[c])

    def e_landed(w, c):
        landed(ein.at[w, e_rows_of(c)], er2.at[c] if w else er.at[c])

    def halo(it, w, way, c):
        device, there_w, _ = targets[w][way]
        source = xin.at[w, rows_of(c)] if it == 0 else x1.at[w, rows_of(c)]
        return (
            source, hbuf.at[it, way, there_w, rows_of(c)], hs.at[((it * 2 + way) * 2 + w) * NCH + c],
            hr.at[((it * 2 + way) * 2 + there_w) * NCH + c], device)

    def halo_start(it, w, c):
        for way in range(2):
            @pl.when(targets[w][way][2])
            def _():
                remote(*halo(it, w, way, c)).start()

    def halo_wait_send(it, w, c):
        for way in range(2):
            @pl.when(targets[w][way][2])
            def _():
                remote(*halo(it, w, way, c)).wait_send()

    def halo_landed(it, w, c):
        for way in range(2):
            @pl.when(targets[w][1 - way][2])
            def _():
                landed(hbuf.at[it, way, w, rows_of(c)], hr.at[((it * 2 + way) * 2 + w) * NCH + c])

    def back(w, c):
        slot = blocks[w][1] % 2
        return (
            hout.at[w, rows_of(c)], hin.at[slot, rows_of(c)], os.at[w * NCH + c], orc.at[slot * NCH + c]), home(*blocks[w])

    for c in range(NCH):
        for s in range(2):
            start(*x_hop(s, c))

    for ta in range(NT):
        for tb in range(NT):
            rows, cols = tile_of(ta), tile_of(tb)
            fe[rows, cols] = fock_ref[rows, cols] * ftile_ref[ta, tb].astype(jnp.float32)
            se[rows, cols] = over_ref[rows, cols] * otile_ref[ta, tb].astype(jnp.float32)
    across = jnp.broadcast_to(ener_ref[...], (NV, NV))
    ener[...] = across + jnp.transpose(across)

    def at_home(s):
        i, j = own[s]
        shift = occ_ref[i, i] + occ_ref[j, j]
        for ta in range(NT):
            e0[s, pl.ds(0, HEAD), tile_of(ta)] = jnp.full((HEAD, TILE), dom_ref[0, s, ta].astype(jnp.float32))
            for tb in range(NT):
                rows, cols = tile_of(ta), tile_of(tb)
                both = (dom_ref[0, s, ta] * dom_ref[0, s, tb]).astype(jnp.float32)
                scale[s, rows, cols] = both / (ener[rows, cols] - shift)
        e0[s, pl.ds(HEAD, NV)] = x_ref[0, s] - scale[s] * k_ref[0, s]

    at_home(0)
    for c in range(NCH):
        landed(xin.at[2, rows_of(c)], xr.at[NCH + c])
        start(*x_relay(c))
    at_home(1)
    for c in range(NCH):
        for s in range(2):
            start(*e_hop(s, c))
    for c in range(NCH):
        x_landed(0, c)
        halo_start(0, 0, c)

    factors = []
    for w, (k, l) in enumerate(blocks):
        lower, upper = jnp.maximum(k - 1, 0), jnp.minimum(k + 1, 31)
        c_own = occ_ref[k, k] * opat_ref[k, k].astype(jnp.float32)
        c_below = occ_ref[k, lower] * opat_ref[k, lower].astype(jnp.float32)
        c_above = occ_ref[k, upper] * opat_ref[k, upper].astype(jnp.float32)
        factors.append((
            c_below * targets[w][1][2].astype(jnp.float32),
            c_above * targets[w][0][2].astype(jnp.float32)))
        mm[w] = fe[...] - c_own * se[...]
        rden[w] = 1.0 / (ener[...] - (occ_ref[k, k] + occ_ref[l, l]))

    def own_part(it, w):
        current = xin[w] if it == 0 else x1[w]
        dd[w] = dot_nn(dot_nt(se[...], current), mm[w])

    def half_residual(it, w):
        c_below, c_above = factors[w]
        for c in range(NCH):
            halo_landed(it, w, c)
            near = c_below * hbuf[it, 0, w, rows_of(c)] + c_above * hbuf[it, 1, w, rows_of(c)]
            vtw[:, rows_of(c)] = dot_nt(se[...], near)
        gt[w] = dd[w] - dot_nn(vtw[...], se[...])

    sources = (pick(diag, 0, 1), pick(diag, 1, 0))

    def both_halves(w, c):
        return jnp.transpose(gt[w, :, rows_of(c)]) + gt[sources[w], rows_of(c)]

    own_part(0, 0)
    for c in range(NCH):
        x_landed(1, c)
        halo_start(0, 1, c)
        landed(ein.at[2, e_rows_of(c)], er.at[NCH + c])
        start(*e_relay(c))
    own_part(0, 1)
    half_residual(0, 0)
    half_residual(0, 1)
    for c in range(NCH):
        for w in range(2):
            e_landed(w, c)
            total = both_halves(w, c)
            hsum[w, rows_of(c)] = total
            for t in range(NT):
                mask = ein[w, pl.ds(0, 1), tile_of(c)] * ein[w, pl.ds(0, 1), tile_of(t)]
                step = mask * rden[w, rows_of(c), tile_of(t)]
                x1[w, rows_of(c), tile_of(t)] = (
                    ein[w, pl.ds(HEAD + c * CH, CH), tile_of(t)] - step * total[:, t * TILE:(t + 1) * TILE])
            halo_start(1, w, c)
    own_part(1, 0)
    own_part(1, 1)
    half_residual(1, 0)
    half_residual(1, 1)
    for c in range(NCH):
        for w in (1, 0):
            hout[w, rows_of(c)] = hsum[w, rows_of(c)] + both_halves(w, c)
            start(*back(w, c))
    for c in range(NCH):
        for s in range(2):
            rows = rows_of(c)
            landed(hin.at[s, rows], orc.at[s * NCH + c])
            out_ref[0, s, rows] = e0[s, pl.ds(HEAD + c * CH, CH)] - scale[s, rows] * (k_ref[0, s, rows] + hin[s, rows])
    for c in range(NCH):
        for s in range(2):
            wait_send(*x_hop(s, c))
            wait_send(*e_hop(s, c))
            wait_send(*back(s, c))
            for it in range(ITERS):
                halo_wait_send(it, s, c)
        wait_send(*x_relay(c))
        wait_send(*e_relay(c))


def shards(
    amplitudes, exchange_ints, virt_fock, intersection, occ_fock, virt_energy, fock_tiles, intersection_tiles,
    occ_pattern, pair_domain,
):
    vmem, smem = pl.BlockSpec(memory_space=pltpu.VMEM), pl.BlockSpec(memory_space=pltpu.SMEM)

    def room(*lead, rows=NV):
        return pltpu.VMEM(lead + (rows, NV), jnp.float32)

    def semaphores(n):
        return pltpu.SemaphoreType.DMA((n * NCH,))

    return pl.pallas_call(
        kernel,
        out_shape=jax.ShapeDtypeStruct(amplitudes.shape, jnp.float32),
        in_specs=[vmem, vmem, vmem, vmem, smem, vmem, smem, smem, smem, smem],
        out_specs=vmem,
        scratch_shapes=[
            room(), room(), room(2), room(),
            room(3), room(3, rows=NV + HEAD), room(2, rows=NV + HEAD),
            room(2), room(2), room(2),
            room(ITERS, 2, 2), room(2), room(2), room(),
            room(2), room(2), room(2),
            semaphores(2), semaphores(2), semaphores(2), semaphores(2),
            semaphores(1), semaphores(1), semaphores(1), semaphores(1),
            semaphores(4 * ITERS), semaphores(4 * ITERS), semaphores(2), semaphores(2),
        ],
        compiler_params=pltpu.CompilerParams(collective_id=0, has_side_effects=True, vmem_limit_bytes=52 * 1024 * 1024),
        cost_estimate=pl.CostEstimate(flops=32 * NV * NV * NV, bytes_accessed=24 * NV * NV, transcendentals=0),
    )(
        amplitudes, exchange_ints, virt_fock, intersection, occ_fock, virt_energy.reshape(1, NV), fock_tiles,
        intersection_tiles, occ_pattern, pair_domain,
    )


def solution(mesh):
    in_specs = (
        P("row", "col", None, None),
        P("row", "col", None, None),
        P(),
        P(),
        P(),
        P(),
        P(),
        P(),
        P(),
        P("row", "col", None),
    )
    out_specs = P("row", "col", None, None)
    return jax.shard_map(shards, mesh=mesh, in_specs=in_specs, out_specs=out_specs, check_vma=False)
```

```python
import jax
import jax.numpy as jnp
from jax import lax
from jax.experimental import pallas as pl
from jax.experimental.pallas import tpu as pltpu
from jax.sharding import PartitionSpec as P

TILE = 128
NT = 3
NV = 384
NCH = 3
CH = NV // NCH
ITERS = 2
HEAD = 8
MESH = pl.DeviceIdType.MESH
HIGHEST = lax.Precision.HIGHEST


def bit(value, place):
    return (value // (1 << place)) % 2


def xor(left, right):
    return (left + right) % 2


def xor3(left, right):
    return sum(xor(bit(left, n), bit(right, n)) * (1 << n) for n in range(3))


def less(left, right):
    return (right - left + 7) // 8


def pick(flag, yes, no):
    return flag * yes + (1 - flag) * no


def parts(index):
    return index // 16, bit(index, 3), index % 8


def is_first(i, j):
    p, u, a = parts(i)
    q, v, b = parts(j)
    near = xor(less(b, a), 1 - u)
    return pick(xor(u, v), u, pick(xor(p, q), xor(p, u), near))


def spot(i, j, zh, zl):
    p, u, a = parts(i)
    q, v, b = parts(j)
    m = xor3(a, b)
    return (2 * xor(u, v) + m // 4) * 8 + zl, zh * 8 + (m % 4) * 2 + xor(p, q)


def manager(i, j):
    first = is_first(i, j)
    zh = pick(first, j // 16, i // 16)
    zl = pick(first, i % 8, j % 8)
    return spot(i, j, zh, zl), 1 - first


def in_plane(i, j):
    return spot(i, j, j // 16, i % 8), 1 - is_first(i, j)


def held(row, col):
    y, a, q = row // 8, row % 8, col // 8
    c, d = y // 2, col % 2
    m = 4 * (y % 2) + (col // 2) % 4
    b = xor3(a, m)
    p = xor(q, d)
    diag = (1 - c) * (1 - d) * ((7 - m) // 7)
    same = pick(d, q, less(b, a))
    u = pick(c, 1, same)
    v = (1 - c) * (same + diag)
    one, two = 16 * p + 8 * u + a, 16 * q + 8 * v + b
    partner = y * 8 + b, p * 8 + col % 8
    return (one, pick(diag, one, two)), (two, pick(diag, two, one)), diag, partner


def home(i, j):
    return i, j // 2


def dot_nt(left, right):
    return lax.dot_general(left, right, (((1,), (1,)), ((), ())), precision=HIGHEST, preferred_element_type=jnp.float32)


def dot_nn(left, right):
    return lax.dot_general(left, right, (((1,), (0,)), ((), ())), precision=HIGHEST, preferred_element_type=jnp.float32)


def rows_of(c):
    return pl.ds(c * CH, CH)


def e_rows_of(c):
    return pl.ds(0, CH + HEAD) if c == 0 else pl.ds(HEAD + c * CH, CH)


def tile_of(t):
    return pl.ds(t * TILE, TILE)


def kernel(
    x_hbm, k_hbm, fock_hbm, over_hbm, occ_hbm, ener_hbm, ftile_hbm, otile_hbm, opat_hbm, dom_hbm,
    hin, scale_hbm, rest_hbm,
    x_ref, k_ref, fock_ref, over_ref, occ_ref, ener_ref, ftile_ref, otile_ref, opat_ref, dom_ref,
    fe, se, mm, ener, xin, ein, e0, scale, rest, rden, x1, hbuf, dd, hsum, hout,
    xs, xr, es, er, xs2, xr2, es2, er2, hs, hr, os, orc, ins, outs,
):
    row = lax.axis_index("row")
    col = lax.axis_index("col")

    def other(device):
        return jnp.logical_or(device[0] != row, device[1] != col)

    loads = [
        pltpu.make_async_copy(source, target, ins.at[n]) for n, (source, target) in enumerate((
            (occ_hbm, occ_ref), (opat_hbm, opat_ref), (ftile_hbm, ftile_ref), (otile_hbm, otile_ref), (dom_hbm, dom_ref),
            (ener_hbm, ener_ref), (fock_hbm, fock_ref), (over_hbm, over_ref), (x_hbm, x_ref), (k_hbm, k_ref)))]
    for load in loads:
        load.start()

    early = is_first(row, 2 * col)
    slots = (early, 1 - early)
    own = [(row, 2 * col + s) for s in slots]
    first_hop = [in_plane(*pair) for pair in own]
    managed_at = [manager(*pair) for pair in own]
    one, two, diag, partner = held(row, col)
    blocks = (one, two)
    relayed = held(*partner)[1]
    targets = []
    for k, l in blocks:
        ways = []
        for step in (1, -1):
            there = jnp.logical_and(k + step >= 0, k + step <= 31)
            device, w = manager(jnp.clip(k + step, 0, 31), l)
            ways.append((device, w, there))
        targets.append(ways)

    barrier = pltpu.get_barrier_semaphore()

    def greet(device, on):
        @pl.when(on)
        def _():
            pl.semaphore_signal(barrier, inc=1, device_id=device, device_id_type=MESH)

    count = jnp.int32(0)
    for device in (home(*one), home(*relayed), partner, managed_at[0][0], managed_at[1][0]):
        greet(device, other(device))
    for device in (first_hop[0][0], first_hop[1][0], partner, home(*one), home(*two)):
        count = count + other(device).astype(jnp.int32)
    for ways in targets:
        for device, _, there in ways:
            greet(device, there)
            count = count + there.astype(jnp.int32)

    for w in range(2):
        for way in range(2):
            @pl.when(jnp.logical_not(targets[w][1 - way][2]))
            def _():
                for it in range(ITERS):
                    hbuf[it, way, w] = jnp.zeros((NV, NV), jnp.float32)

    pl.semaphore_wait(barrier, count)

    def remote(source, target, send, recv, device):
        return pltpu.make_async_remote_copy(
            src_ref=source, dst_ref=target, send_sem=send, recv_sem=recv, device_id=device, device_id_type=MESH)

    def start(args, device):
        @pl.when(other(device))
        def _():
            remote(*args, device).start()

        @pl.when(jnp.logical_not(other(device)))
        def _():
            pltpu.make_async_copy(args[0], args[1], args[3]).start()

    def wait_send(args, device):
        @pl.when(other(device))
        def _():
            remote(*args, device).wait_send()

    def landed(buffer, semaphore):
        pltpu.make_async_copy(buffer, buffer, semaphore).wait()

    def x_hop(n, c):
        device, w = first_hop[n]
        return (x_hbm.at[0, slots[n], rows_of(c)], xin.at[2 * w, rows_of(c)], xs.at[n * NCH + c], xr.at[w * NCH + c]), device

    def e_hop(n, c):
        device, w = first_hop[n]
        return (e0.at[n, e_rows_of(c)], ein.at[2 * w, e_rows_of(c)], es.at[n * NCH + c], er.at[w * NCH + c]), device

    def x_relay(c):
        return (xin.at[2, rows_of(c)], xin.at[1, rows_of(c)], xs2.at[c], xr2.at[c]), partner

    def e_relay(c):
        return (ein.at[2, e_rows_of(c)], ein.at[1, e_rows_of(c)], es2.at[c], er2.at[c]), partner

    def x_landed(w, c):
        landed(xin.at[w, rows_of(c)], xr2.at[c] if w else xr.at[c])

    def e_landed(w, c):
        landed(ein.at[w, e_rows_of(c)], er2.at[c] if w else er.at[c])

    def halo(it, w, way, c):
        device, there_w, _ = targets[w][way]
        source = xin.at[w, rows_of(c)] if it == 0 else x1.at[w, rows_of(c)]
        return (
            source, hbuf.at[it, way, there_w, rows_of(c)], hs.at[((it * 2 + way) * 2 + w) * NCH + c],
            hr.at[((it * 2 + way) * 2 + there_w) * NCH + c], device)

    def halo_start(it, w, c):
        for way in range(2):
            @pl.when(targets[w][way][2])
            def _():
                remote(*halo(it, w, way, c)).start()

    def halo_wait_send(it, w, c):
        for way in range(2):
            @pl.when(targets[w][way][2])
            def _():
                remote(*halo(it, w, way, c)).wait_send()

    def halo_landed(it, w, c):
        for way in range(2):
            @pl.when(targets[w][1 - way][2])
            def _():
                landed(hbuf.at[it, way, w, rows_of(c)], hr.at[((it * 2 + way) * 2 + w) * NCH + c])

    def back(w, c):
        slot = blocks[w][1] % 2
        return (
            hout.at[w, rows_of(c)], hin.at[0, slot, rows_of(c)], os.at[w * NCH + c], orc.at[slot * NCH + c]), home(*blocks[w])

    for n in range(2):
        for c in range(NCH):
            start(*x_hop(n, c))
    for load in loads:
        load.wait()

    for ta in range(NT):
        for tb in range(NT):
            rows, cols = tile_of(ta), tile_of(tb)
            fe[rows, cols] = fock_ref[rows, cols] * ftile_ref[ta, tb].astype(jnp.float32)
            se[rows, cols] = over_ref[rows, cols] * otile_ref[ta, tb].astype(jnp.float32)
    across = jnp.broadcast_to(ener_ref[...], (NV, NV))
    ener[...] = across + jnp.transpose(across)

    def at_home(n):
        (i, j), s = own[n], slots[n]
        shift = occ_ref[i, i] + occ_ref[j, j]
        for ta in range(NT):
            e0[n, pl.ds(0, HEAD), tile_of(ta)] = jnp.full((HEAD, TILE), dom_ref[0, s, ta].astype(jnp.float32))
            for tb in range(NT):
                rows, cols = tile_of(ta), tile_of(tb)
                both = (dom_ref[0, s, ta] * dom_ref[0, s, tb]).astype(jnp.float32)
                scale[n, rows, cols] = both / (ener[rows, cols] - shift)
        exchange = scale[n] * k_ref[0, s]
        once = x_ref[0, s] - exchange
        e0[n, pl.ds(HEAD, NV)] = once
        rest[n] = once - exchange

    def keep(n):
        return (
            pltpu.make_async_copy(scale.at[n], scale_hbm.at[0, slots[n]], outs.at[2 * n]),
            pltpu.make_async_copy(rest.at[n], rest_hbm.at[0, slots[n]], outs.at[2 * n + 1]))

    at_home(0)
    for c in range(NCH):
        landed(xin.at[2, rows_of(c)], xr.at[NCH + c])
        start(*x_relay(c))
    for c in range(NCH):
        start(*e_hop(0, c))
    at_home(1)
    for c in range(NCH):
        start(*e_hop(1, c))
    for c in range(NCH):
        x_landed(0, c)
        halo_start(0, 0, c)

    factors = []
    for w, (k, l) in enumerate(blocks):
        lower, upper = jnp.maximum(k - 1, 0), jnp.minimum(k + 1, 31)
        c_own = occ_ref[k, k] * opat_ref[k, k].astype(jnp.float32)
        c_below = occ_ref[k, lower] * opat_ref[k, lower].astype(jnp.float32)
        c_above = occ_ref[k, upper] * opat_ref[k, upper].astype(jnp.float32)
        factors.append((
            c_below * targets[w][1][2].astype(jnp.float32),
            c_above * targets[w][0][2].astype(jnp.float32)))
        mm[w] = fe[...] - c_own * se[...]
        rden[w] = 1.0 / (ener[...] - (occ_ref[k, k] + occ_ref[l, l]))

    def own_part(it, w):
        current = xin[w] if it == 0 else x1[w]
        dd[w] = dot_nn(dot_nt(se[...], current), mm[w])

    def near_part(it):
        for c in range(NCH):
            for w in range(2):
                c_below, c_above = factors[w]
                halo_landed(it, w, c)
                near = c_below * hbuf[it, 0, w, rows_of(c)] + c_above * hbuf[it, 1, w, rows_of(c)]
                dd[w] = dd[w] - dot_nn(dot_nt(se[...], near), se[rows_of(c)])

    sources = (pick(diag, 0, 1), pick(diag, 1, 0))

    def both_halves(w, c):
        return jnp.transpose(dd[w, :, rows_of(c)]) + dd[sources[w], rows_of(c)]

    own_part(0, 0)
    for c in range(NCH):
        x_landed(1, c)
        halo_start(0, 1, c)
        landed(ein.at[2, e_rows_of(c)], er.at[NCH + c])
        start(*e_relay(c))
    own_part(0, 1)
    near_part(0)
    for c in range(NCH):
        for w in range(2):
            e_landed(w, c)
            total = both_halves(w, c)
            hsum[w, rows_of(c)] = total
            for t in range(NT):
                mask = ein[w, pl.ds(0, 1), tile_of(c)] * ein[w, pl.ds(0, 1), tile_of(t)]
                step = mask * rden[w, rows_of(c), tile_of(t)]
                x1[w, rows_of(c), tile_of(t)] = (
                    ein[w, pl.ds(HEAD + c * CH, CH), tile_of(t)] - step * total[:, t * TILE:(t + 1) * TILE])
            halo_start(1, w, c)
    own_part(1, 0)
    own_part(1, 1)
    for n in range(2):
        for copy in keep(n):
            copy.start()
    near_part(1)
    for c in range(NCH):
        for w in (1, 0):
            hout[w, rows_of(c)] = hsum[w, rows_of(c)] + both_halves(w, c)
            start(*back(w, c))
    for c in range(NCH):
        for s in range(2):
            landed(hin.at[0, s, rows_of(c)], orc.at[s * NCH + c])
    for n in range(2):
        for copy in keep(n):
            copy.wait()
    for c in range(NCH):
        for s in range(2):
            wait_send(*x_hop(s, c))
            wait_send(*e_hop(s, c))
            wait_send(*back(s, c))
            for it in range(ITERS):
                halo_wait_send(it, s, c)
        wait_send(*x_relay(c))
        wait_send(*e_relay(c))


def shards(
    amplitudes, exchange_ints, virt_fock, intersection, occ_fock, virt_energy, fock_tiles, intersection_tiles,
    occ_pattern, pair_domain,
):
    def room(*lead, rows=NV):
        return pltpu.VMEM(lead + (rows, NV), jnp.float32)

    def semaphores(n):
        return pltpu.SemaphoreType.DMA((n * NCH,))

    whole = jax.ShapeDtypeStruct(amplitudes.shape, jnp.float32)
    later, scale, rest = pl.pallas_call(
        kernel,
        out_shape=(whole, whole, whole),
        in_specs=[pl.BlockSpec(memory_space=pl.ANY)] * 10,
        out_specs=(pl.BlockSpec(memory_space=pl.ANY),) * 3,
        scratch_shapes=[
            pltpu.VMEM(amplitudes.shape, jnp.float32), pltpu.VMEM(amplitudes.shape, jnp.float32), room(), room(),
            pltpu.SMEM(occ_fock.shape, jnp.float32), pltpu.VMEM((1, NV), jnp.float32),
            pltpu.SMEM((NT, NT), jnp.int32), pltpu.SMEM((NT, NT), jnp.int32),
            pltpu.SMEM(occ_pattern.shape, jnp.int32), pltpu.SMEM(pair_domain.shape, jnp.int32),
            room(), room(), room(2), room(),
            room(3), room(3, rows=NV + HEAD), room(2, rows=NV + HEAD),
            room(2), room(2), room(2), room(2),
            room(ITERS, 2, 2), room(2),
            room(2), room(2),
            semaphores(2), semaphores(2), semaphores(2), semaphores(2),
            semaphores(1), semaphores(1), semaphores(1), semaphores(1),
            semaphores(4 * ITERS), semaphores(4 * ITERS), semaphores(2), semaphores(2),
            pltpu.SemaphoreType.DMA((10,)), pltpu.SemaphoreType.DMA((4,)),
        ],
        compiler_params=pltpu.CompilerParams(collective_id=0, has_side_effects=True, vmem_limit_bytes=60 * 1024 * 1024),
        cost_estimate=pl.CostEstimate(flops=32 * NV * NV * NV, bytes_accessed=24 * NV * NV, transcendentals=0),
    )(
        amplitudes, exchange_ints, virt_fock, intersection, occ_fock, virt_energy.reshape(1, NV), fock_tiles,
        intersection_tiles, occ_pattern, pair_domain,
    )
    return rest - scale * later


def solution(mesh):
    in_specs = (
        P("row", "col", None, None),
        P("row", "col", None, None),
        P(),
        P(),
        P(),
        P(),
        P(),
        P(),
        P(),
        P("row", "col", None),
    )
    out_specs = P("row", "col", None, None)
    return jax.shard_map(shards, mesh=mesh, in_specs=in_specs, out_specs=out_specs, check_vma=False)
```

```python
import jax
import jax.numpy as jnp
from jax import lax
from jax.experimental import pallas as pl
from jax.experimental.pallas import tpu as pltpu
from jax.sharding import PartitionSpec as P

TILE = 128
NT = 3
NV = 384
NCH = 3
CH = NV // NCH
ITERS = 2
HEAD = 8
MESH = pl.DeviceIdType.MESH
HIGHEST = lax.Precision.HIGHEST


def bit(value, place):
    return (value // (1 << place)) % 2


def xor(left, right):
    return (left + right) % 2


def xor3(left, right):
    return sum(xor(bit(left, n), bit(right, n)) * (1 << n) for n in range(3))


def less(left, right):
    return (right - left + 7) // 8


def pick(flag, yes, no):
    return flag * yes + (1 - flag) * no


def parts(index):
    return index // 16, bit(index, 3), index % 8


def is_first(i, j):
    p, u, a = parts(i)
    q, v, b = parts(j)
    near = xor(less(b, a), 1 - u)
    return pick(xor(u, v), xor(u, (1 - p) * (1 - q)), pick(xor(p, q), xor(p, u), near))


def spot(i, j, zh, zl):
    p, u, a = parts(i)
    q, v, b = parts(j)
    m = xor3(a, b)
    return (2 * xor(u, v) + m // 4) * 8 + zl, zh * 8 + (m % 4) * 2 + xor(p, q)


def manager(i, j):
    first = is_first(i, j)
    zh = pick(first, j // 16, i // 16)
    zl = pick(first, i % 8, j % 8)
    return spot(i, j, zh, zl), 1 - first


def in_plane(i, j):
    return spot(i, j, j // 16, i % 8), 1 - is_first(i, j)


def held(row, col):
    y, a, q = row // 8, row % 8, col // 8
    c, d = y // 2, col % 2
    m = 4 * (y % 2) + (col // 2) % 4
    b = xor3(a, m)
    p = xor(q, d)
    diag = (1 - c) * (1 - d) * ((7 - m) // 7)
    same = pick(d, q, less(b, a))
    apart = 1 - (1 - d) * (1 - q)
    u = pick(c, apart, same)
    v = pick(c, 1 - apart, same + diag)
    one, two = 16 * p + 8 * u + a, 16 * q + 8 * v + b
    partner = y * 8 + b, p * 8 + col % 8
    return (one, pick(diag, one, two)), (two, pick(diag, two, one)), diag, partner


def home(i, j):
    return i, j // 2


def dot_nt(left, right):
    return lax.dot_general(left, right, (((1,), (1,)), ((), ())), precision=HIGHEST, preferred_element_type=jnp.float32)


def dot_nn(left, right):
    return lax.dot_general(left, right, (((1,), (0,)), ((), ())), precision=HIGHEST, preferred_element_type=jnp.float32)


def rows_of(c):
    return pl.ds(c * CH, CH)


def e_rows_of(c):
    return pl.ds(0, CH + HEAD) if c == 0 else pl.ds(HEAD + c * CH, CH)


def tile_of(t):
    return pl.ds(t * TILE, TILE)


def kernel(
    x_hbm, k_hbm, fock_hbm, over_hbm, occ_hbm, ener_hbm, ftile_hbm, otile_hbm, opat_hbm, dom_hbm,
    hin, scale_hbm, rest_hbm,
    x_ref, k_ref, fock_ref, over_ref, occ_ref, ener_ref, ftile_ref, otile_ref, opat_ref, dom_ref,
    fe, se, mm, ener, xin, ein, e0, scale, rest, rden, x1, hbuf, dd, hsum, hout,
    xs, xr, es, er, xs2, xr2, es2, er2, hs, hr, os, orc, ins, outs,
):
    row = lax.axis_index("row")
    col = lax.axis_index("col")

    def other(device):
        return jnp.logical_or(device[0] != row, device[1] != col)

    loads = [
        pltpu.make_async_copy(source, target, ins.at[n]) for n, (source, target) in enumerate((
            (occ_hbm, occ_ref), (opat_hbm, opat_ref), (ftile_hbm, ftile_ref), (otile_hbm, otile_ref), (dom_hbm, dom_ref),
            (ener_hbm, ener_ref), (fock_hbm, fock_ref), (over_hbm, over_ref), (x_hbm, x_ref), (k_hbm, k_ref)))]
    for load in loads:
        load.start()

    slots = (0, 1)
    own = [(row, 2 * col + s) for s in slots]
    first_hop = [in_plane(*pair) for pair in own]
    managed_at = [manager(*pair) for pair in own]
    one, two, diag, partner = held(row, col)
    blocks = (one, two)
    relayed = held(*partner)[1]
    targets = []
    for k, l in blocks:
        ways = []
        for step in (1, -1):
            there = jnp.logical_and(k + step >= 0, k + step <= 31)
            device, w = manager(jnp.clip(k + step, 0, 31), l)
            planes = (device[1] // 8 - col // 8) * 8 + device[0] % 8 - row % 8
            far = (planes + 17) % 16 > 2
            ways.append((device, w, there, far))
        targets.append(ways)

    barrier = pltpu.get_barrier_semaphore()

    def greet(device, on):
        @pl.when(on)
        def _():
            pl.semaphore_signal(barrier, inc=1, device_id=device, device_id_type=MESH)

    count = jnp.int32(0)
    for device in (home(*one), home(*relayed), partner, managed_at[0][0], managed_at[1][0]):
        greet(device, other(device))
    for device in (first_hop[0][0], first_hop[1][0], partner, home(*one), home(*two)):
        count = count + other(device).astype(jnp.int32)
    for ways in targets:
        for device, _, there, _ in ways:
            greet(device, there)
            count = count + there.astype(jnp.int32)

    for w in range(2):
        for way in range(2):
            @pl.when(jnp.logical_not(targets[w][1 - way][2]))
            def _():
                for it in range(ITERS):
                    hbuf[it, way, w] = jnp.zeros((NV, NV), jnp.float32)

    pl.semaphore_wait(barrier, count)

    def remote(source, target, send, recv, device):
        return pltpu.make_async_remote_copy(
            src_ref=source, dst_ref=target, send_sem=send, recv_sem=recv, device_id=device, device_id_type=MESH)

    def start(args, device):
        @pl.when(other(device))
        def _():
            remote(*args, device).start()

        @pl.when(jnp.logical_not(other(device)))
        def _():
            pltpu.make_async_copy(args[0], args[1], args[3]).start()

    def wait_send(args, device):
        @pl.when(other(device))
        def _():
            remote(*args, device).wait_send()

    def landed(buffer, semaphore):
        pltpu.make_async_copy(buffer, buffer, semaphore).wait()

    def x_hop(n, c):
        device, w = first_hop[n]
        return (x_hbm.at[0, slots[n], rows_of(c)], xin.at[2 * w, rows_of(c)], xs.at[n * NCH + c], xr.at[w * NCH + c]), device

    def e_hop(n, c):
        device, w = first_hop[n]
        return (e0.at[n, e_rows_of(c)], ein.at[2 * w, e_rows_of(c)], es.at[n * NCH + c], er.at[w * NCH + c]), device

    def x_relay(c):
        return (xin.at[2, rows_of(c)], xin.at[1, rows_of(c)], xs2.at[c], xr2.at[c]), partner

    def e_relay(c):
        return (ein.at[2, e_rows_of(c)], ein.at[1, e_rows_of(c)], es2.at[c], er2.at[c]), partner

    def x_landed(w, c):
        landed(xin.at[w, rows_of(c)], xr2.at[c] if w else xr.at[c])

    def e_landed(w, c):
        landed(ein.at[w, e_rows_of(c)], er2.at[c] if w else er.at[c])

    def halo(it, w, way, c):
        device, there_w, _, _ = targets[w][way]
        source = xin.at[w, rows_of(c)] if it == 0 else x1.at[w, rows_of(c)]
        return (
            source, hbuf.at[it, way, there_w, rows_of(c)], hs.at[((it * 2 + way) * 2 + w) * NCH + c],
            hr.at[((it * 2 + way) * 2 + there_w) * NCH + c], device)

    def halo_start(it, w, c, which=None):
        for way in range(2):
            _, _, there, far = targets[w][way]
            if which is not None:
                there = jnp.logical_and(there, far if which == "far" else jnp.logical_not(far))

            @pl.when(there)
            def _():
                remote(*halo(it, w, way, c)).start()

    def halo_wait_send(it, w, c):
        for way in range(2):
            @pl.when(targets[w][way][2])
            def _():
                remote(*halo(it, w, way, c)).wait_send()

    def halo_landed(it, w, c):
        for way in range(2):
            @pl.when(targets[w][1 - way][2])
            def _():
                landed(hbuf.at[it, way, w, rows_of(c)], hr.at[((it * 2 + way) * 2 + w) * NCH + c])

    def back(w, c):
        slot = blocks[w][1] % 2
        return (
            hout.at[w, rows_of(c)], hin.at[0, slot, rows_of(c)], os.at[w * NCH + c], orc.at[slot * NCH + c]), home(*blocks[w])

    def hops(hop, kind):
        for c in range(NCH):
            for n in range(2):
                @pl.when(first_hop[n][1] == kind)
                def _():
                    start(*hop(n, c))

    hops(x_hop, 1)
    for load in loads:
        load.wait()

    for ta in range(NT):
        for tb in range(NT):
            rows, cols = tile_of(ta), tile_of(tb)
            fe[rows, cols] = fock_ref[rows, cols] * ftile_ref[ta, tb].astype(jnp.float32)
            se[rows, cols] = over_ref[rows, cols] * otile_ref[ta, tb].astype(jnp.float32)
    across = jnp.broadcast_to(ener_ref[...], (NV, NV))
    ener[...] = across + jnp.transpose(across)

    def at_home(n):
        (i, j), s = own[n], slots[n]
        shift = occ_ref[i, i] + occ_ref[j, j]
        for ta in range(NT):
            e0[n, pl.ds(0, HEAD), tile_of(ta)] = jnp.full((HEAD, TILE), dom_ref[0, s, ta].astype(jnp.float32))
            for tb in range(NT):
                rows, cols = tile_of(ta), tile_of(tb)
                both = (dom_ref[0, s, ta] * dom_ref[0, s, tb]).astype(jnp.float32)
                scale[n, rows, cols] = both / (ener[rows, cols] - shift)
        exchange = scale[n] * k_ref[0, s]
        once = x_ref[0, s] - exchange
        e0[n, pl.ds(HEAD, NV)] = once
        rest[n] = once - exchange

    def keep(n):
        return (
            pltpu.make_async_copy(scale.at[n], scale_hbm.at[0, slots[n]], outs.at[2 * n]),
            pltpu.make_async_copy(rest.at[n], rest_hbm.at[0, slots[n]], outs.at[2 * n + 1]))

    for c in range(NCH):
        landed(xin.at[2, rows_of(c)], xr.at[NCH + c])
        start(*x_relay(c))
    hops(x_hop, 0)
    at_home(0)
    at_home(1)
    hops(e_hop, 1)
    for c in range(NCH):
        x_landed(0, c)
        halo_start(0, 0, c, "far")
    for c in range(NCH):
        wait_send(*x_relay(c))
    for c in range(NCH):
        halo_start(0, 0, c, "near")
    hops(e_hop, 0)

    factors = []
    for w, (k, l) in enumerate(blocks):
        lower, upper = jnp.maximum(k - 1, 0), jnp.minimum(k + 1, 31)
        c_own = occ_ref[k, k] * opat_ref[k, k].astype(jnp.float32)
        c_below = occ_ref[k, lower] * opat_ref[k, lower].astype(jnp.float32)
        c_above = occ_ref[k, upper] * opat_ref[k, upper].astype(jnp.float32)
        factors.append((
            c_below * targets[w][1][2].astype(jnp.float32),
            c_above * targets[w][0][2].astype(jnp.float32)))
        mm[w] = fe[...] - c_own * se[...]
        rden[w] = 1.0 / (ener[...] - (occ_ref[k, k] + occ_ref[l, l]))

    def own_part(it, w):
        current = xin[w] if it == 0 else x1[w]
        dd[w] = dot_nn(dot_nt(se[...], current), mm[w])

    def near_part(it):
        for c in range(NCH):
            for w in range(2):
                c_below, c_above = factors[w]
                halo_landed(it, w, c)
                near = c_below * hbuf[it, 0, w, rows_of(c)] + c_above * hbuf[it, 1, w, rows_of(c)]
                dd[w] = dd[w] - dot_nn(dot_nt(se[...], near), se[rows_of(c)])

    sources = (pick(diag, 0, 1), pick(diag, 1, 0))

    def both_halves(w, c):
        return jnp.transpose(dd[w, :, rows_of(c)]) + dd[sources[w], rows_of(c)]

    own_part(0, 0)
    for c in range(NCH):
        x_landed(1, c)
        halo_start(0, 1, c)
    for c in range(NCH):
        landed(ein.at[2, e_rows_of(c)], er.at[NCH + c])
        start(*e_relay(c))
    own_part(0, 1)
    near_part(0)
    for c in range(NCH):
        for w in range(2):
            e_landed(w, c)
            total = both_halves(w, c)
            hsum[w, rows_of(c)] = total
            for t in range(NT):
                mask = ein[w, pl.ds(0, 1), tile_of(c)] * ein[w, pl.ds(0, 1), tile_of(t)]
                step = mask * rden[w, rows_of(c), tile_of(t)]
                x1[w, rows_of(c), tile_of(t)] = (
                    ein[w, pl.ds(HEAD + c * CH, CH), tile_of(t)] - step * total[:, t * TILE:(t + 1) * TILE])
            halo_start(1, w, c)
    own_part(1, 0)
    own_part(1, 1)
    for n in range(2):
        for copy in keep(n):
            copy.start()
    near_part(1)
    for c in range(NCH):
        for w in (1, 0):
            hout[w, rows_of(c)] = hsum[w, rows_of(c)] + both_halves(w, c)
            start(*back(w, c))
    for c in range(NCH):
        for s in range(2):
            landed(hin.at[0, s, rows_of(c)], orc.at[s * NCH + c])
    for n in range(2):
        for copy in keep(n):
            copy.wait()
    for c in range(NCH):
        for s in range(2):
            wait_send(*x_hop(s, c))
            wait_send(*e_hop(s, c))
            wait_send(*back(s, c))
            for it in range(ITERS):
                halo_wait_send(it, s, c)
        wait_send(*e_relay(c))


def shards(
    amplitudes, exchange_ints, virt_fock, intersection, occ_fock, virt_energy, fock_tiles, intersection_tiles,
    occ_pattern, pair_domain,
):
    def room(*lead, rows=NV):
        return pltpu.VMEM(lead + (rows, NV), jnp.float32)

    def semaphores(n):
        return pltpu.SemaphoreType.DMA((n * NCH,))

    whole = jax.ShapeDtypeStruct(amplitudes.shape, jnp.float32)
    later, scale, rest = pl.pallas_call(
        kernel,
        out_shape=(whole, whole, whole),
        in_specs=[pl.BlockSpec(memory_space=pl.ANY)] * 10,
        out_specs=(pl.BlockSpec(memory_space=pl.ANY),) * 3,
        scratch_shapes=[
            pltpu.VMEM(amplitudes.shape, jnp.float32), pltpu.VMEM(amplitudes.shape, jnp.float32), room(), room(),
            pltpu.SMEM(occ_fock.shape, jnp.float32), pltpu.VMEM((1, NV), jnp.float32),
            pltpu.SMEM((NT, NT), jnp.int32), pltpu.SMEM((NT, NT), jnp.int32),
            pltpu.SMEM(occ_pattern.shape, jnp.int32), pltpu.SMEM(pair_domain.shape, jnp.int32),
            room(), room(), room(2), room(),
            room(3), room(3, rows=NV + HEAD), room(2, rows=NV + HEAD),
            room(2), room(2), room(2), room(2),
            room(ITERS, 2, 2), room(2),
            room(2), room(2),
            semaphores(2), semaphores(2), semaphores(2), semaphores(2),
            semaphores(1), semaphores(1), semaphores(1), semaphores(1),
            semaphores(4 * ITERS), semaphores(4 * ITERS), semaphores(2), semaphores(2),
            pltpu.SemaphoreType.DMA((10,)), pltpu.SemaphoreType.DMA((4,)),
        ],
        compiler_params=pltpu.CompilerParams(collective_id=0, has_side_effects=True, vmem_limit_bytes=60 * 1024 * 1024),
        cost_estimate=pl.CostEstimate(flops=32 * NV * NV * NV, bytes_accessed=24 * NV * NV, transcendentals=0),
    )(
        amplitudes, exchange_ints, virt_fock, intersection, occ_fock, virt_energy.reshape(1, NV), fock_tiles,
        intersection_tiles, occ_pattern, pair_domain,
    )
    return rest - scale * later


def solution(mesh):
    in_specs = (
        P("row", "col", None, None),
        P("row", "col", None, None),
        P(),
        P(),
        P(),
        P(),
        P(),
        P(),
        P(),
        P("row", "col", None),
    )
    out_specs = P("row", "col", None, None)
    return jax.shard_map(shards, mesh=mesh, in_specs=in_specs, out_specs=out_specs, check_vma=False)
```

```python
import jax
import jax.numpy as jnp
from jax import lax
from jax.experimental import pallas as pl
from jax.experimental.pallas import tpu as pltpu
from jax.sharding import PartitionSpec as P

TILE = 128
NT = 3
NV = 384
NCH = 3
CH = NV // NCH
ITERS = 2
HEAD = 8
DIRECT = (0, 1)
MESH = pl.DeviceIdType.MESH
HIGHEST = lax.Precision.HIGHEST


def bit(value, place):
    return (value // (1 << place)) % 2


def xor(left, right):
    return (left + right) % 2


def xor3(left, right):
    return sum(xor(bit(left, n), bit(right, n)) * (1 << n) for n in range(3))


def less(left, right):
    return (right - left + 7) // 8


def pick(flag, yes, no):
    return flag * yes + (1 - flag) * no


def parts(index):
    return index // 16, bit(index, 3), index % 8


def is_first(i, j):
    p, u, a = parts(i)
    q, v, b = parts(j)
    near = xor(less(b, a), 1 - u)
    return pick(xor(u, v), xor(u, (1 - p) * (1 - q)), pick(xor(p, q), xor(p, u), near))


def spot(i, j, zh, zl):
    p, u, a = parts(i)
    q, v, b = parts(j)
    m = xor3(a, b)
    return (2 * xor(u, v) + m // 4) * 8 + zl, zh * 8 + (m % 4) * 2 + xor(p, q)


def manager(i, j):
    first = is_first(i, j)
    zh = pick(first, j // 16, i // 16)
    zl = pick(first, i % 8, j % 8)
    return spot(i, j, zh, zl), 1 - first


def in_plane(i, j):
    return spot(i, j, j // 16, i % 8), 1 - is_first(i, j)


def held(row, col):
    y, a, q = row // 8, row % 8, col // 8
    c, d = y // 2, col % 2
    m = 4 * (y % 2) + (col // 2) % 4
    b = xor3(a, m)
    p = xor(q, d)
    diag = (1 - c) * (1 - d) * ((7 - m) // 7)
    same = pick(d, q, less(b, a))
    apart = 1 - (1 - d) * (1 - q)
    u = pick(c, apart, same)
    v = pick(c, 1 - apart, same + diag)
    one, two = 16 * p + 8 * u + a, 16 * q + 8 * v + b
    partner = y * 8 + b, p * 8 + col % 8
    return (one, pick(diag, one, two)), (two, pick(diag, two, one)), diag, partner


def home(i, j):
    return i, j // 2


def dot_nt(left, right):
    return lax.dot_general(left, right, (((1,), (1,)), ((), ())), precision=HIGHEST, preferred_element_type=jnp.float32)


def dot_nn(left, right):
    return lax.dot_general(left, right, (((1,), (0,)), ((), ())), precision=HIGHEST, preferred_element_type=jnp.float32)


def rows_of(c):
    return pl.ds(c * CH, CH)


def e_rows_of(c):
    return pl.ds(0, CH + HEAD) if c == 0 else pl.ds(HEAD + c * CH, CH)


def tile_of(t):
    return pl.ds(t * TILE, TILE)


def kernel(
    x_hbm, k_hbm, fock_hbm, over_hbm, occ_hbm, ener_hbm, ftile_hbm, otile_hbm, opat_hbm, dom_hbm,
    hin, scale_hbm, rest_hbm,
    x_ref, k_ref, fock_ref, over_ref, occ_ref, ener_ref, ftile_ref, otile_ref, opat_ref, dom_ref,
    fe, se, mm, ener, xin, ein, e0, scale, rest, rden, x1, hbuf, dd, hsum, hout,
    xs, xr, es, er, xs2, xr2, es2, er2, hs, hr, ds, os, orc, ins, outs,
):
    row = lax.axis_index("row")
    col = lax.axis_index("col")

    def other(device):
        return jnp.logical_or(device[0] != row, device[1] != col)

    loads = [
        pltpu.make_async_copy(source, target, ins.at[n]) for n, (source, target) in enumerate((
            (occ_hbm, occ_ref), (opat_hbm, opat_ref), (ftile_hbm, ftile_ref), (otile_hbm, otile_ref), (dom_hbm, dom_ref),
            (ener_hbm, ener_ref), (fock_hbm, fock_ref), (over_hbm, over_ref), (x_hbm, x_ref), (k_hbm, k_ref)))]
    for load in loads:
        load.start()

    slots = (0, 1)
    own = [(row, 2 * col + s) for s in slots]
    first_hop = [in_plane(*pair) for pair in own]
    managed_at = [manager(*pair) for pair in own]
    one, two, diag, partner = held(row, col)
    blocks = (one, two)
    relayed = held(*partner)[1]
    def both_ways(k, l):
        ways = []
        for step in (1, -1):
            there = jnp.logical_and(k + step >= 0, k + step <= 31)
            device, w = manager(jnp.clip(k + step, 0, 31), l)
            planes = (device[1] // 8 - col // 8) * 8 + device[0] % 8 - row % 8
            far = (planes + 17) % 16 > 2
            ways.append((device, w, there, far))
        return ways

    targets = [both_ways(k, l) for k, l in blocks]
    direct = []
    for pair, (_, kind) in zip(own, first_hop):
        direct.append([
            (device, w, jnp.logical_and(kind == 0, jnp.logical_and(there, jnp.logical_not(far))))
            for device, w, there, far in both_ways(*pair)])

    barrier = pltpu.get_barrier_semaphore()

    def greet(device, on):
        @pl.when(on)
        def _():
            pl.semaphore_signal(barrier, inc=1, device_id=device, device_id_type=MESH)

    count = jnp.int32(0)
    for device in (home(*one), home(*relayed), partner, managed_at[0][0], managed_at[1][0]):
        greet(device, other(device))
    for device in (first_hop[0][0], first_hop[1][0], partner, home(*one), home(*two)):
        count = count + other(device).astype(jnp.int32)
    for (k, l), ways in zip(blocks, targets):
        for (device, w, there, far), step in zip(ways, (1, -1)):
            greet(device, there)
            count = count + there.astype(jnp.int32)
            source = home(jnp.clip(k + step, 0, 31), l)
            sends = jnp.logical_and(w == 0, jnp.logical_and(there, jnp.logical_not(far)))
            greet(source, jnp.logical_and(sends, other(source)))
    for ways in direct:
        for device, _, on in ways:
            count = count + jnp.logical_and(on, other(device)).astype(jnp.int32)

    for w in range(2):
        for way in range(2):
            @pl.when(jnp.logical_not(targets[w][1 - way][2]))
            def _():
                for it in range(ITERS):
                    hbuf[it, way, w] = jnp.zeros((NV, NV), jnp.float32)

    pl.semaphore_wait(barrier, count)

    def remote(source, target, send, recv, device):
        return pltpu.make_async_remote_copy(
            src_ref=source, dst_ref=target, send_sem=send, recv_sem=recv, device_id=device, device_id_type=MESH)

    def start(args, device):
        @pl.when(other(device))
        def _():
            remote(*args, device).start()

        @pl.when(jnp.logical_not(other(device)))
        def _():
            pltpu.make_async_copy(args[0], args[1], args[3]).start()

    def wait_send(args, device):
        @pl.when(other(device))
        def _():
            remote(*args, device).wait_send()

    def landed(buffer, semaphore):
        pltpu.make_async_copy(buffer, buffer, semaphore).wait()

    def x_hop(n, c):
        device, w = first_hop[n]
        return (x_hbm.at[0, slots[n], rows_of(c)], xin.at[2 * w, rows_of(c)], xs.at[n * NCH + c], xr.at[w * NCH + c]), device

    def e_hop(n, c):
        device, w = first_hop[n]
        return (e0.at[n, e_rows_of(c)], ein.at[2 * w, e_rows_of(c)], es.at[n * NCH + c], er.at[w * NCH + c]), device

    def x_relay(c):
        return (xin.at[2, rows_of(c)], xin.at[1, rows_of(c)], xs2.at[c], xr2.at[c]), partner

    def e_relay(c):
        return (ein.at[2, e_rows_of(c)], ein.at[1, e_rows_of(c)], es2.at[c], er2.at[c]), partner

    def x_landed(w, c):
        landed(xin.at[w, rows_of(c)], xr2.at[c] if w else xr.at[c])

    def e_landed(w, c):
        landed(ein.at[w, e_rows_of(c)], er2.at[c] if w else er.at[c])

    def halo(it, w, way, c):
        device, there_w, _, _ = targets[w][way]
        source = xin.at[w, rows_of(c)] if it == 0 else x1.at[w, rows_of(c)]
        return (
            source, hbuf.at[it, way, there_w, rows_of(c)], hs.at[((it * 2 + way) * 2 + w) * NCH + c],
            hr.at[((it * 2 + way) * 2 + there_w) * NCH + c], device)

    def halo_start(it, w, c, which=None):
        for way in range(2):
            _, _, there, far = targets[w][way]
            if which is not None:
                there = jnp.logical_and(there, far if which == "far" else jnp.logical_not(far))

            @pl.when(there)
            def _():
                remote(*halo(it, w, way, c)).start()

    def halo_wait_send(it, w, c):
        for way in range(2):
            _, _, there, far = targets[w][way]
            if it == 0 and w == 0 and c in DIRECT:
                there = jnp.logical_and(there, far)

            @pl.when(there)
            def _():
                remote(*halo(it, w, way, c)).wait_send()

    def direct_halo(n, way, c):
        device, there_w, _ = direct[n][way]
        return (
            x_hbm.at[0, n, rows_of(c)], hbuf.at[0, way, there_w, rows_of(c)], ds.at[(n * 2 + way) * NCH + c],
            hr.at[(way * 2 + there_w) * NCH + c]), device

    def each_direct(act):
        for c in DIRECT:
            for n in range(2):
                for way in range(2):
                    @pl.when(direct[n][way][2])
                    def _():
                        act(*direct_halo(n, way, c))

    def halo_landed(it, w, c):
        for way in range(2):
            @pl.when(targets[w][1 - way][2])
            def _():
                landed(hbuf.at[it, way, w, rows_of(c)], hr.at[((it * 2 + way) * 2 + w) * NCH + c])

    def back(w, c):
        slot = blocks[w][1] % 2
        return (
            hout.at[w, rows_of(c)], hin.at[0, slot, rows_of(c)], os.at[w * NCH + c], orc.at[slot * NCH + c]), home(*blocks[w])

    def hops(hop, kind):
        for c in range(NCH):
            for n in range(2):
                @pl.when(first_hop[n][1] == kind)
                def _():
                    start(*hop(n, c))

    hops(x_hop, 1)
    each_direct(start)
    for load in loads:
        load.wait()

    for ta in range(NT):
        for tb in range(NT):
            rows, cols = tile_of(ta), tile_of(tb)
            fe[rows, cols] = fock_ref[rows, cols] * ftile_ref[ta, tb].astype(jnp.float32)
            se[rows, cols] = over_ref[rows, cols] * otile_ref[ta, tb].astype(jnp.float32)
    across = jnp.broadcast_to(ener_ref[...][None, :], (NV, NV))
    ener[...] = across + jnp.transpose(across)

    def at_home(n):
        (i, j), s = own[n], slots[n]
        shift = occ_ref[i, i] + occ_ref[j, j]
        for ta in range(NT):
            e0[n, pl.ds(0, HEAD), tile_of(ta)] = jnp.full((HEAD, TILE), dom_ref[0, s, ta].astype(jnp.float32))
            for tb in range(NT):
                rows, cols = tile_of(ta), tile_of(tb)
                both = (dom_ref[0, s, ta] * dom_ref[0, s, tb]).astype(jnp.float32)
                scale[n, rows, cols] = both / (ener[rows, cols] - shift)
        exchange = scale[n] * k_ref[0, s]
        once = x_ref[0, s] - exchange
        e0[n, pl.ds(HEAD, NV)] = once
        rest[n] = once - exchange

    def keep(n):
        return (
            pltpu.make_async_copy(scale.at[n], scale_hbm.at[0, slots[n]], outs.at[2 * n]),
            pltpu.make_async_copy(rest.at[n], rest_hbm.at[0, slots[n]], outs.at[2 * n + 1]))

    for c in range(NCH):
        landed(xin.at[2, rows_of(c)], xr.at[NCH + c])
        start(*x_relay(c))
    hops(x_hop, 0)
    at_home(0)
    at_home(1)
    hops(e_hop, 1)
    for c in range(NCH):
        x_landed(0, c)
        halo_start(0, 0, c, "far")
    for c in range(NCH):
        wait_send(*x_relay(c))
    for c in range(NCH):
        if c not in DIRECT:
            halo_start(0, 0, c, "near")
    hops(e_hop, 0)

    factors = []
    for w, (k, l) in enumerate(blocks):
        lower, upper = jnp.maximum(k - 1, 0), jnp.minimum(k + 1, 31)
        c_own = occ_ref[k, k] * opat_ref[k, k].astype(jnp.float32)
        c_below = occ_ref[k, lower] * opat_ref[k, lower].astype(jnp.float32)
        c_above = occ_ref[k, upper] * opat_ref[k, upper].astype(jnp.float32)
        factors.append((
            c_below * targets[w][1][2].astype(jnp.float32),
            c_above * targets[w][0][2].astype(jnp.float32)))
        mm[w] = fe[...] - c_own * se[...]
        rden[w] = 1.0 / (ener[...] - (occ_ref[k, k] + occ_ref[l, l]))

    def own_part(it, w):
        current = xin[w] if it == 0 else x1[w]
        dd[w] = dot_nn(dot_nt(se[...], current), mm[w])

    def near_part(it):
        for c in range(NCH):
            for w in range(2):
                c_below, c_above = factors[w]
                halo_landed(it, w, c)
                near = c_below * hbuf[it, 0, w, rows_of(c)] + c_above * hbuf[it, 1, w, rows_of(c)]
                dd[w] = dd[w] - dot_nn(dot_nt(se[...], near), se[rows_of(c)])

    sources = (pick(diag, 0, 1), pick(diag, 1, 0))

    def both_halves(w, c):
        return jnp.transpose(dd[w, :, rows_of(c)]) + dd[sources[w], rows_of(c)]

    own_part(0, 0)
    for c in range(NCH):
        x_landed(1, c)
        halo_start(0, 1, c)
    for c in range(NCH):
        landed(ein.at[2, e_rows_of(c)], er.at[NCH + c])
        start(*e_relay(c))
    own_part(0, 1)
    near_part(0)
    for c in range(NCH):
        for w in range(2):
            e_landed(w, c)
            total = both_halves(w, c)
            hsum[w, rows_of(c)] = total
            for t in range(NT):
                mask = ein[w, pl.ds(0, 1), tile_of(c)] * ein[w, pl.ds(0, 1), tile_of(t)]
                step = mask * rden[w, rows_of(c), tile_of(t)]
                x1[w, rows_of(c), tile_of(t)] = (
                    ein[w, pl.ds(HEAD + c * CH, CH), tile_of(t)] - step * total[:, t * TILE:(t + 1) * TILE])
            halo_start(1, w, c)
    own_part(1, 0)
    own_part(1, 1)
    for n in range(2):
        for copy in keep(n):
            copy.start()
    near_part(1)
    for c in range(NCH):
        for w in (1, 0):
            hout[w, rows_of(c)] = hsum[w, rows_of(c)] + both_halves(w, c)
            start(*back(w, c))
    for c in range(NCH):
        for s in range(2):
            landed(hin.at[0, s, rows_of(c)], orc.at[s * NCH + c])
    for n in range(2):
        for copy in keep(n):
            copy.wait()
    each_direct(wait_send)
    for c in range(NCH):
        for s in range(2):
            wait_send(*x_hop(s, c))
            wait_send(*e_hop(s, c))
            wait_send(*back(s, c))
            for it in range(ITERS):
                halo_wait_send(it, s, c)
        wait_send(*e_relay(c))


def shards(
    amplitudes, exchange_ints, virt_fock, intersection, occ_fock, virt_energy, fock_tiles, intersection_tiles,
    occ_pattern, pair_domain,
):
    def room(*lead, rows=NV):
        return pltpu.VMEM(lead + (rows, NV), jnp.float32)

    def semaphores(n):
        return pltpu.SemaphoreType.DMA((n * NCH,))

    whole = jax.ShapeDtypeStruct(amplitudes.shape, jnp.float32)
    later, scale, rest = pl.pallas_call(
        kernel,
        out_shape=(whole, whole, whole),
        in_specs=[pl.BlockSpec(memory_space=pl.ANY)] * 10,
        out_specs=(pl.BlockSpec(memory_space=pl.ANY),) * 3,
        scratch_shapes=[
            pltpu.VMEM(amplitudes.shape, jnp.float32), pltpu.VMEM(amplitudes.shape, jnp.float32), room(), room(),
            pltpu.SMEM(occ_fock.shape, jnp.float32), pltpu.VMEM((NV,), jnp.float32),
            pltpu.SMEM((NT, NT), jnp.int32), pltpu.SMEM((NT, NT), jnp.int32),
            pltpu.SMEM(occ_pattern.shape, jnp.int32), pltpu.SMEM(pair_domain.shape, jnp.int32),
            room(), room(), room(2), room(),
            room(3), room(3, rows=NV + HEAD), room(2, rows=NV + HEAD),
            room(2), room(2), room(2), room(2),
            room(ITERS, 2, 2), room(2),
            room(2), room(2),
            semaphores(2), semaphores(2), semaphores(2), semaphores(2),
            semaphores(1), semaphores(1), semaphores(1), semaphores(1),
            semaphores(4 * ITERS), semaphores(4 * ITERS), semaphores(4), semaphores(2), semaphores(2),
            pltpu.SemaphoreType.DMA((10,)), pltpu.SemaphoreType.DMA((4,)),
        ],
        compiler_params=pltpu.CompilerParams(collective_id=0, has_side_effects=True, vmem_limit_bytes=60 * 1024 * 1024),
        cost_estimate=pl.CostEstimate(flops=32 * NV * NV * NV, bytes_accessed=24 * NV * NV, transcendentals=0),
    )(
        amplitudes, exchange_ints, virt_fock, intersection, occ_fock, virt_energy, fock_tiles,
        intersection_tiles, occ_pattern, pair_domain,
    )
    return rest - scale * later


def solution(mesh):
    in_specs = (
        P("row", "col", None, None),
        P("row", "col", None, None),
        P(),
        P(),
        P(),
        P(),
        P(),
        P(),
        P(),
        P("row", "col", None),
    )
    out_specs = P("row", "col", None, None)
    return jax.shard_map(shards, mesh=mesh, in_specs=in_specs, out_specs=out_specs, check_vma=False)
```

```python
import jax
import jax.numpy as jnp
from jax import lax
from jax.experimental import pallas as pl
from jax.experimental.pallas import tpu as pltpu
from jax.sharding import PartitionSpec as P

TILE = 128
NT = 3
NV = 384
NCH = 3
CH = NV // NCH
ITERS = 2
HEAD = 8
DIRECT = (0,)
MESH = pl.DeviceIdType.MESH
HIGHEST = lax.Precision.HIGHEST


def bit(value, place):
    return (value // (1 << place)) % 2


def xor(left, right):
    return (left + right) % 2


def xor3(left, right):
    return sum(xor(bit(left, n), bit(right, n)) * (1 << n) for n in range(3))


def less(left, right):
    return (right - left + 7) // 8


def pick(flag, yes, no):
    return flag * yes + (1 - flag) * no


def parts(index):
    return index // 16, bit(index, 3), index % 8


def is_first(i, j):
    p, u, a = parts(i)
    q, v, b = parts(j)
    near = xor(less(b, a), 1 - u)
    return pick(xor(u, v), xor(u, (1 - p) * (1 - q)), pick(xor(p, q), xor(p, u), near))


def spot(i, j, zh, zl):
    p, u, a = parts(i)
    q, v, b = parts(j)
    m = xor3(a, b)
    return (2 * xor(u, v) + m // 4) * 8 + zl, zh * 8 + (m % 4) * 2 + xor(p, q)


def manager(i, j):
    first = is_first(i, j)
    zh = pick(first, j // 16, i // 16)
    zl = pick(first, i % 8, j % 8)
    return spot(i, j, zh, zl), 1 - first


def in_plane(i, j):
    return spot(i, j, j // 16, i % 8), 1 - is_first(i, j)


def held(row, col):
    y, a, q = row // 8, row % 8, col // 8
    c, d = y // 2, col % 2
    m = 4 * (y % 2) + (col // 2) % 4
    b = xor3(a, m)
    p = xor(q, d)
    diag = (1 - c) * (1 - d) * ((7 - m) // 7)
    same = pick(d, q, less(b, a))
    apart = 1 - (1 - d) * (1 - q)
    u = pick(c, apart, same)
    v = pick(c, 1 - apart, same + diag)
    one, two = 16 * p + 8 * u + a, 16 * q + 8 * v + b
    partner = y * 8 + b, p * 8 + col % 8
    return (one, pick(diag, one, two)), (two, pick(diag, two, one)), diag, partner


def home(i, j):
    return i, j // 2


def dot_nt(left, right):
    return lax.dot_general(left, right, (((1,), (1,)), ((), ())), precision=HIGHEST, preferred_element_type=jnp.float32)


def dot_nn(left, right):
    return lax.dot_general(left, right, (((1,), (0,)), ((), ())), precision=HIGHEST, preferred_element_type=jnp.float32)


def rows_of(c):
    return pl.ds(c * CH, CH)


def e_rows_of(c):
    return pl.ds(0, CH + HEAD) if c == 0 else pl.ds(HEAD + c * CH, CH)


def tile_of(t):
    return pl.ds(t * TILE, TILE)


def kernel(
    x_hbm, k_hbm, fock_hbm, over_hbm, occ_hbm, ener_hbm, ftile_hbm, otile_hbm, opat_hbm, dom_hbm,
    hin, scale_hbm, rest_hbm,
    x_ref, k_ref, fock_ref, over_ref, occ_ref, ener_ref, ftile_ref, otile_ref, opat_ref, dom_ref,
    fe, se, mm, ener, xin, ein, e0, scale, rest, rden, x1, hbuf, dd, hsum, hout,
    xs, xr, es, er, xs2, xr2, es2, er2, hs, hr, ds, os, orc, ins, outs,
):
    row = lax.axis_index("row")
    col = lax.axis_index("col")

    def other(device):
        return jnp.logical_or(device[0] != row, device[1] != col)

    loads = [
        pltpu.make_async_copy(source, target, ins.at[n]) for n, (source, target) in enumerate((
            (occ_hbm, occ_ref), (opat_hbm, opat_ref), (ftile_hbm, ftile_ref), (otile_hbm, otile_ref), (dom_hbm, dom_ref),
            (ener_hbm, ener_ref), (fock_hbm, fock_ref), (over_hbm, over_ref), (x_hbm, x_ref), (k_hbm, k_ref)))]
    for load in loads:
        load.start()

    slots = (0, 1)
    own = [(row, 2 * col + s) for s in slots]
    first_hop = [in_plane(*pair) for pair in own]
    managed_at = [manager(*pair) for pair in own]
    one, two, diag, partner = held(row, col)
    blocks = (one, two)
    relayed = held(*partner)[1]
    def both_ways(k, l):
        ways = []
        for step in (1, -1):
            there = jnp.logical_and(k + step >= 0, k + step <= 31)
            device, w = manager(jnp.clip(k + step, 0, 31), l)
            planes = (device[1] // 8 - col // 8) * 8 + device[0] % 8 - row % 8
            far = (planes + 17) % 16 > 2
            ways.append((device, w, there, far))
        return ways

    targets = [both_ways(k, l) for k, l in blocks]
    direct = []
    for pair, (_, kind) in zip(own, first_hop):
        direct.append([
            (device, w, jnp.logical_and(kind == 0, jnp.logical_and(there, jnp.logical_not(far))))
            for device, w, there, far in both_ways(*pair)])

    barrier = pltpu.get_barrier_semaphore()

    def greet(device, on):
        @pl.when(on)
        def _():
            pl.semaphore_signal(barrier, inc=1, device_id=device, device_id_type=MESH)

    count = jnp.int32(0)
    for device in (home(*one), home(*relayed), partner, managed_at[0][0], managed_at[1][0]):
        greet(device, other(device))
    for device in (first_hop[0][0], first_hop[1][0], partner, home(*one), home(*two)):
        count = count + other(device).astype(jnp.int32)
    for (k, l), ways in zip(blocks, targets):
        for (device, w, there, far), step in zip(ways, (1, -1)):
            greet(device, there)
            count = count + there.astype(jnp.int32)
            source = home(jnp.clip(k + step, 0, 31), l)
            sends = jnp.logical_and(w == 0, jnp.logical_and(there, jnp.logical_not(far)))
            greet(source, jnp.logical_and(sends, other(source)))
    for ways in direct:
        for device, _, on in ways:
            count = count + jnp.logical_and(on, other(device)).astype(jnp.int32)

    for w in range(2):
        for way in range(2):
            @pl.when(jnp.logical_not(targets[w][1 - way][2]))
            def _():
                for it in range(ITERS):
                    hbuf[it, way, w] = jnp.zeros((NV, NV), jnp.float32)

    pl.semaphore_wait(barrier, count)

    def remote(source, target, send, recv, device):
        return pltpu.make_async_remote_copy(
            src_ref=source, dst_ref=target, send_sem=send, recv_sem=recv, device_id=device, device_id_type=MESH)

    def start(args, device):
        @pl.when(other(device))
        def _():
            remote(*args, device).start()

        @pl.when(jnp.logical_not(other(device)))
        def _():
            pltpu.make_async_copy(args[0], args[1], args[3]).start()

    def wait_send(args, device):
        @pl.when(other(device))
        def _():
            remote(*args, device).wait_send()

    def landed(buffer, semaphore):
        pltpu.make_async_copy(buffer, buffer, semaphore).wait()

    def x_hop(n, c):
        device, w = first_hop[n]
        return (x_hbm.at[0, slots[n], rows_of(c)], xin.at[2 * w, rows_of(c)], xs.at[n * NCH + c], xr.at[w * NCH + c]), device

    def e_hop(n, c):
        device, w = first_hop[n]
        return (e0.at[n, e_rows_of(c)], ein.at[2 * w, e_rows_of(c)], es.at[n * NCH + c], er.at[w * NCH + c]), device

    def x_relay(c):
        return (xin.at[2, rows_of(c)], xin.at[1, rows_of(c)], xs2.at[c], xr2.at[c]), partner

    def e_relay(c):
        return (ein.at[2, e_rows_of(c)], ein.at[1, e_rows_of(c)], es2.at[c], er2.at[c]), partner

    def x_landed(w, c):
        landed(xin.at[w, rows_of(c)], xr2.at[c] if w else xr.at[c])

    def e_landed(w, c):
        landed(ein.at[w, e_rows_of(c)], er2.at[c] if w else er.at[c])

    def halo(it, w, way, c):
        device, there_w, _, _ = targets[w][way]
        source = xin.at[w, rows_of(c)] if it == 0 else x1.at[w, rows_of(c)]
        return (
            source, hbuf.at[it, way, there_w, rows_of(c)], hs.at[((it * 2 + way) * 2 + w) * NCH + c],
            hr.at[((it * 2 + way) * 2 + there_w) * NCH + c], device)

    def halo_start(it, w, c, only_far=False):
        for way in range(2):
            _, _, there, far = targets[w][way]
            if only_far:
                there = jnp.logical_and(there, far)

            @pl.when(there)
            def _():
                remote(*halo(it, w, way, c)).start()

    def halo_wait_send(it, w, c):
        for way in range(2):
            _, _, there, far = targets[w][way]
            if it == 0 and w == 0 and c in DIRECT:
                there = jnp.logical_and(there, far)

            @pl.when(there)
            def _():
                remote(*halo(it, w, way, c)).wait_send()

    def direct_halo(n, way, c):
        device, there_w, _ = direct[n][way]
        return (
            x_hbm.at[0, n, rows_of(c)], hbuf.at[0, way, there_w, rows_of(c)], ds.at[(n * 2 + way) * NCH + c],
            hr.at[(way * 2 + there_w) * NCH + c]), device

    def each_direct(act):
        for c in DIRECT:
            for n in range(2):
                for way in range(2):
                    @pl.when(direct[n][way][2])
                    def _():
                        act(*direct_halo(n, way, c))

    def halo_landed(it, w, c):
        for way in range(2):
            @pl.when(targets[w][1 - way][2])
            def _():
                landed(hbuf.at[it, way, w, rows_of(c)], hr.at[((it * 2 + way) * 2 + w) * NCH + c])

    def back(w, c):
        slot = blocks[w][1] % 2
        return (
            hout.at[w, rows_of(c)], hin.at[0, slot, rows_of(c)], os.at[w * NCH + c], orc.at[slot * NCH + c]), home(*blocks[w])

    def hops(hop, kind):
        for c in range(NCH):
            for n in range(2):
                @pl.when(first_hop[n][1] == kind)
                def _():
                    start(*hop(n, c))

    hops(x_hop, 1)
    each_direct(start)
    for load in loads:
        load.wait()

    for ta in range(NT):
        for tb in range(NT):
            rows, cols = tile_of(ta), tile_of(tb)
            fe[rows, cols] = fock_ref[rows, cols] * ftile_ref[ta, tb].astype(jnp.float32)
            se[rows, cols] = over_ref[rows, cols] * otile_ref[ta, tb].astype(jnp.float32)
    across = jnp.broadcast_to(ener_ref[...][None, :], (NV, NV))
    ener[...] = across + jnp.transpose(across)

    def at_home(n):
        (i, j), s = own[n], slots[n]
        shift = occ_ref[i, i] + occ_ref[j, j]
        for ta in range(NT):
            e0[n, pl.ds(0, HEAD), tile_of(ta)] = jnp.full((HEAD, TILE), dom_ref[0, s, ta].astype(jnp.float32))
            for tb in range(NT):
                rows, cols = tile_of(ta), tile_of(tb)
                both = (dom_ref[0, s, ta] * dom_ref[0, s, tb]).astype(jnp.float32)
                scale[n, rows, cols] = both / (ener[rows, cols] - shift)
        exchange = scale[n] * k_ref[0, s]
        once = x_ref[0, s] - exchange
        e0[n, pl.ds(HEAD, NV)] = once
        rest[n] = once - exchange

    def keep(n):
        return (
            pltpu.make_async_copy(scale.at[n], scale_hbm.at[0, slots[n]], outs.at[2 * n]),
            pltpu.make_async_copy(rest.at[n], rest_hbm.at[0, slots[n]], outs.at[2 * n + 1]))

    for c in range(NCH):
        landed(xin.at[2, rows_of(c)], xr.at[NCH + c])
        start(*x_relay(c))
    hops(x_hop, 0)
    at_home(0)
    at_home(1)
    hops(e_hop, 1)
    for c in range(NCH):
        x_landed(0, c)
        halo_start(0, 0, c, only_far=c in DIRECT)

    factors = []
    for w, (k, l) in enumerate(blocks):
        lower, upper = jnp.maximum(k - 1, 0), jnp.minimum(k + 1, 31)
        c_own = occ_ref[k, k] * opat_ref[k, k].astype(jnp.float32)
        c_below = occ_ref[k, lower] * opat_ref[k, lower].astype(jnp.float32)
        c_above = occ_ref[k, upper] * opat_ref[k, upper].astype(jnp.float32)
        factors.append((
            c_below * targets[w][1][2].astype(jnp.float32),
            c_above * targets[w][0][2].astype(jnp.float32)))
        mm[w] = fe[...] - c_own * se[...]
        rden[w] = 1.0 / (ener[...] - (occ_ref[k, k] + occ_ref[l, l]))

    def own_part(it, w):
        current = xin[w] if it == 0 else x1[w]
        dd[w] = dot_nn(dot_nt(se[...], current), mm[w])

    def near_part(it):
        for c in range(NCH):
            for w in range(2):
                c_below, c_above = factors[w]
                halo_landed(it, w, c)
                near = c_below * hbuf[it, 0, w, rows_of(c)] + c_above * hbuf[it, 1, w, rows_of(c)]
                dd[w] = dd[w] - dot_nn(dot_nt(se[...], near), se[rows_of(c)])

    sources = (pick(diag, 0, 1), pick(diag, 1, 0))

    def both_halves(w, c):
        return jnp.transpose(dd[w, :, rows_of(c)]) + dd[sources[w], rows_of(c)]

    own_part(0, 0)
    for c in range(NCH):
        x_landed(1, c)
        halo_start(0, 1, c)
    for c in range(NCH):
        landed(ein.at[2, e_rows_of(c)], er.at[NCH + c])
        start(*e_relay(c))
    hops(e_hop, 0)
    own_part(0, 1)
    near_part(0)
    for c in range(NCH):
        for w in range(2):
            e_landed(w, c)
            total = both_halves(w, c)
            hsum[w, rows_of(c)] = total
            for t in range(NT):
                mask = ein[w, pl.ds(0, 1), tile_of(c)] * ein[w, pl.ds(0, 1), tile_of(t)]
                step = mask * rden[w, rows_of(c), tile_of(t)]
                x1[w, rows_of(c), tile_of(t)] = (
                    ein[w, pl.ds(HEAD + c * CH, CH), tile_of(t)] - step * total[:, t * TILE:(t + 1) * TILE])
            halo_start(1, w, c)
    own_part(1, 0)
    own_part(1, 1)
    for n in range(2):
        for copy in keep(n):
            copy.start()
    near_part(1)
    for c in range(NCH):
        for w in (1, 0):
            hout[w, rows_of(c)] = hsum[w, rows_of(c)] + both_halves(w, c)
            start(*back(w, c))
    for c in range(NCH):
        for s in range(2):
            landed(hin.at[0, s, rows_of(c)], orc.at[s * NCH + c])
    for n in range(2):
        for copy in keep(n):
            copy.wait()
    each_direct(wait_send)
    for c in range(NCH):
        for s in range(2):
            wait_send(*x_hop(s, c))
            wait_send(*e_hop(s, c))
            wait_send(*back(s, c))
            for it in range(ITERS):
                halo_wait_send(it, s, c)
        wait_send(*x_relay(c))
        wait_send(*e_relay(c))


def shards(
    amplitudes, exchange_ints, virt_fock, intersection, occ_fock, virt_energy, fock_tiles, intersection_tiles,
    occ_pattern, pair_domain,
):
    def room(*lead, rows=NV):
        return pltpu.VMEM(lead + (rows, NV), jnp.float32)

    def semaphores(n):
        return pltpu.SemaphoreType.DMA((n * NCH,))

    whole = jax.ShapeDtypeStruct(amplitudes.shape, jnp.float32)
    later, scale, rest = pl.pallas_call(
        kernel,
        out_shape=(whole, whole, whole),
        in_specs=[pl.BlockSpec(memory_space=pl.ANY)] * 10,
        out_specs=(pl.BlockSpec(memory_space=pl.ANY),) * 3,
        scratch_shapes=[
            pltpu.VMEM(amplitudes.shape, jnp.float32), pltpu.VMEM(amplitudes.shape, jnp.float32), room(), room(),
            pltpu.SMEM(occ_fock.shape, jnp.float32), pltpu.VMEM((NV,), jnp.float32),
            pltpu.SMEM((NT, NT), jnp.int32), pltpu.SMEM((NT, NT), jnp.int32),
            pltpu.SMEM(occ_pattern.shape, jnp.int32), pltpu.SMEM(pair_domain.shape, jnp.int32),
            room(), room(), room(2), room(),
            room(3), room(3, rows=NV + HEAD), room(2, rows=NV + HEAD),
            room(2), room(2), room(2), room(2),
            room(ITERS, 2, 2), room(2),
            room(2), room(2),
            semaphores(2), semaphores(2), semaphores(2), semaphores(2),
            semaphores(1), semaphores(1), semaphores(1), semaphores(1),
            semaphores(4 * ITERS), semaphores(4 * ITERS), semaphores(4), semaphores(2), semaphores(2),
            pltpu.SemaphoreType.DMA((10,)), pltpu.SemaphoreType.DMA((4,)),
        ],
        compiler_params=pltpu.CompilerParams(collective_id=0, has_side_effects=True, vmem_limit_bytes=60 * 1024 * 1024),
        cost_estimate=pl.CostEstimate(flops=32 * NV * NV * NV, bytes_accessed=24 * NV * NV, transcendentals=0),
    )(
        amplitudes, exchange_ints, virt_fock, intersection, occ_fock, virt_energy, fock_tiles,
        intersection_tiles, occ_pattern, pair_domain,
    )
    return rest - scale * later


def solution(mesh):
    in_specs = (
        P("row", "col", None, None),
        P("row", "col", None, None),
        P(),
        P(),
        P(),
        P(),
        P(),
        P(),
        P(),
        P("row", "col", None),
    )
    out_specs = P("row", "col", None, None)
    return jax.shard_map(shards, mesh=mesh, in_specs=in_specs, out_specs=out_specs, check_vma=False)
```
